512 devices in a mesh: blk: 8 (over z_hi, core), dp: 64 (over z_lo, x, y).
Axes of the slice: x: 4, y: 8, z: 8 (z_hi: 4, z_lo: 2; z = z_hi * 2 + z_lo), core: 2. Of those that a mesh axis runs over, the one named last changes fastest.
Arguments:
- audio_features: bfloat16 [131072, 1024], P(('blk', 'dp'))
- proj_weight: bfloat16 [1024, 512], replicated
- text_raw: bfloat16 [131072, 512], P(('blk', 'dp'))
- positive: int32 [131072], P(('blk', 'dp')), may hold values from 0 to 2047
Outputs:
- grad_weight: float32 [1024, 512], replicated
- grad_features: bfloat16 [131072, 1024], P(('blk', 'dp'))
- grad_text: float32 [131072, 512], P(('blk', 'dp'))
The draws below stay inside these ranges and needn't reach their ends.
Inputs may be any that keep to these rules, and one draw needn't show every extreme that they name: Any text row of a group may be the positive of several audio rows of that group or of none.
All inputs are finite; a program needn't handle non-finite values.
Results may differ from the reference program's by a relative error of at most 0.015.
Values may be sent and summed in bfloat16 or wider, within the bound.
No kernel may reach another device: no remote copies, remote signals or barrier semaphores. Data moves between devices by JAX's collectives and lax.ppermute only.
A program may use at most 64 MiB of HBM per device.

```python
import jax
import jax.numpy as jnp
from jax import lax

C = 1024
E = 512
ROWS = 256
GROUP = 2048
TOKENS = 131072
N_BLK = 8
N_DP = 64


def shared_parts(key):
    key_weight = jax.random.fold_in(key, 0)
    weight = jax.random.normal(key_weight, (C, E), jnp.float32) * (1.0 / C ** 0.5)
    return weight


def draw_proj_weight(key, part):
    weight = shared_parts(key)
    return weight.astype(jnp.bfloat16)


def draw_text_raw(key, part):
    key = jax.random.fold_in(key, 11)
    values = jax.random.normal(key, (TOKENS, E), jnp.float32)
    return values.astype(jnp.bfloat16)


def draw_audio_features(key, part):
    key = jax.random.fold_in(key, 23)
    values = jax.random.normal(key, (TOKENS, C), jnp.float32)
    return values.astype(jnp.bfloat16)


def set_ends(drawn, stream_key, smallest, high):
    spot = [jax.random.randint(jax.random.fold_in(stream_key, axis), (), 0, length) for axis, length in enumerate(drawn.shape)]
    widest = drawn.shape.index(max(drawn.shape))
    beside = spot[:widest] + [(spot[widest] + 1) % drawn.shape[widest]] + spot[widest + 1:]
    return drawn.at[tuple(spot)].set(smallest).at[tuple(beside)].set(high)


def setup_inputs(seed: int = 0) -> dict:
    key_list = jax.random.split(jax.random.key(seed), 5)
    audio_features = draw_audio_features(jax.random.fold_in(key_list[4], 71), 0)
    proj_weight = draw_proj_weight(jax.random.fold_in(key_list[4], 71), 0)
    text_raw = draw_text_raw(jax.random.fold_in(key_list[4], 71), 0)
    positive = set_ends(jax.random.randint(key_list[3], (TOKENS,), 0, GROUP), jax.random.fold_in(key_list[3], 1), 0, GROUP - 1).astype(jnp.int32)
    return dict(audio_features=audio_features, proj_weight=proj_weight, text_raw=text_raw, positive=positive)


SCALE = 100.0
EPS = 1e-06

def to_groups(values):
    width = values.shape[-1]
    return values.reshape(N_BLK, N_DP, ROWS, width).transpose(1, 0, 2, 3).reshape(N_DP, GROUP, width)

def from_groups(values):
    width = values.shape[-1]
    return values.reshape(N_DP, N_BLK, ROWS, width).transpose(1, 0, 2, 3).reshape(TOKENS, width)

def reference(audio_features, proj_weight, text_raw, positive):
    proj = jnp.dot(audio_features, proj_weight, preferred_element_type=jnp.float32)
    audio_scale = lax.rsqrt(lax.optimization_barrier(jnp.sum(proj * proj, axis=1, keepdims=True)) + EPS)
    audio = proj * audio_scale
    audio_b = audio.astype(jnp.bfloat16)
    text_f = text_raw.astype(jnp.float32)
    text_scale = lax.rsqrt(lax.optimization_barrier(jnp.sum(text_f * text_f, axis=1, keepdims=True)) + EPS)
    text = text_f * text_scale
    text_b = text.astype(jnp.bfloat16)
    columns = jnp.arange(GROUP, dtype=jnp.int32)
    pos_groups = to_groups(positive.reshape(TOKENS, 1))[:, :, 0]

    def one_group(item):
        aud, txt, pos = item
        scores = SCALE * jnp.dot(aud, txt.T, preferred_element_type=jnp.float32)
        peak = lax.optimization_barrier(jnp.max(scores, axis=1, keepdims=True))
        lse = peak + jnp.log(lax.optimization_barrier(jnp.sum(jnp.exp(scores - peak), axis=1, keepdims=True)))
        match = jnp.where(pos[:, None] == columns[None, :], 1.0, 0.0)
        grads = (jnp.exp(scores - lse) - match).astype(jnp.bfloat16)
        audio_part = SCALE * jnp.dot(grads, txt, preferred_element_type=jnp.float32)
        text_part = SCALE * jnp.dot(grads.T, aud, preferred_element_type=jnp.float32)
        return (audio_part, text_part)
    audio_parts, text_parts = lax.map(one_group, (to_groups(audio_b), to_groups(text_b), pos_groups))
    audio_grad = from_groups(audio_parts)
    text_grad = from_groups(text_parts)
    along = lax.optimization_barrier(jnp.sum(audio * audio_grad, axis=1, keepdims=True))
    proj_grad = ((audio_grad - audio * along) * audio_scale).astype(jnp.bfloat16)
    grad_features = jnp.dot(proj_grad, proj_weight.T, preferred_element_type=jnp.float32).astype(jnp.bfloat16)
    grad_weight = jnp.dot(audio_features.T, proj_grad, preferred_element_type=jnp.float32)
    text_along = lax.optimization_barrier(jnp.sum(text * text_grad, axis=1, keepdims=True))
    grad_text = (text_grad - text * text_along) * text_scale
    return (grad_weight, grad_features, grad_text)
```

```python
import jax
import jax.numpy as jnp
from jax import lax
from jax.sharding import Mesh, PartitionSpec as P

SCALE = 100.0
EPS = 1e-06
FINE = ("zh", "core", "zl", "x", "y")
PLANE = ("x", "y")
COLUMN = ("zh", "zl")


def shifted(block, axis, distance):
    count = lax.axis_size(axis)
    return lax.ppermute(block, axis, [(i, (i + distance) % count) for i in range(count)])


def exchanged(block, axes):
    return lax.all_to_all(block, axes, split_axis=0, concat_axis=0, tiled=True)


def copies(block, count):
    return jnp.broadcast_to(block[None], (count,) + block.shape).reshape(
        (count * block.shape[0],) + block.shape[1:]
    )


def folded(block, count):
    parts = block.reshape((count, block.shape[0] // count) + block.shape[1:])
    return jnp.sum(parts.astype(jnp.float32), axis=0)


def dot(a, b, da, db):
    return lax.dot_general(a, b, (((da,), (db,)), ((), ())), preferred_element_type=jnp.float32)


def summed_everywhere(own, other):
    core = lax.axis_index("core")
    plane = lax.axis_size(PLANE)
    column = lax.axis_size(COLUMN)
    half = (own + shifted(other.astype(jnp.bfloat16), "core", 1)).astype(jnp.bfloat16)
    part = folded(exchanged(half, PLANE), plane).astype(jnp.bfloat16)
    part = folded(exchanged(copies(part, column), COLUMN), column).astype(jnp.bfloat16)
    half = exchanged(copies(part, plane), PLANE)
    there = shifted(half, "core", 1)
    low = jnp.where(core == 0, half, there)
    high = jnp.where(core == 0, there, half)
    return jnp.concatenate([low, high]).astype(jnp.float32)


def body(audio_features, proj_weight, text_raw, positive):
    rows = audio_features.shape[0]
    width = text_raw.shape[1]
    channels = audio_features.shape[1]
    chips = lax.axis_size("zh")
    cores = lax.axis_size("core")
    core = lax.axis_index("core")
    chip = lax.axis_index("zh")
    text_f = text_raw.astype(jnp.float32)
    text_scale = lax.rsqrt(jnp.sum(text_f * text_f, axis=1, keepdims=True) + EPS)
    text = text_f * text_scale
    text_b = text.astype(jnp.bfloat16)
    mine = [text_b] + [shifted(text_b, "zh", k) for k in range(1, chips)]
    beside = [shifted(piece, "core", 1) for piece in mine]
    proj = dot(audio_features, proj_weight, 1, 0)
    audio_scale = lax.rsqrt(jnp.sum(proj * proj, axis=1, keepdims=True) + EPS)
    audio = proj * audio_scale
    audio_b = audio.astype(jnp.bfloat16)
    pieces = mine + beside
    offsets = jnp.arange(rows, dtype=jnp.int32)
    scores = [SCALE * dot(audio_b, piece, 1, 1) for piece in pieces]
    peak = jnp.max(jnp.stack([jnp.max(s, axis=1) for s in scores]), axis=0)
    total = sum(jnp.sum(jnp.exp(s - peak[:, None]), axis=1) for s in scores)
    lse = peak + jnp.log(total)
    tiles = []
    for n, s in enumerate(scores):
        column = core if n < chips else 1 - core
        block = (chip - n % chips + chips) % chips * cores + column
        ids = block * rows + offsets
        match = jnp.where(positive[:, None] == ids[None, :], 1.0, 0.0)
        tiles.append((jnp.exp(s - lse[:, None]) - match).astype(jnp.bfloat16))
    audio_grad = SCALE * sum(dot(tile, piece, 1, 0) for tile, piece in zip(tiles, pieces))
    along = jnp.sum(audio * audio_grad, axis=1, keepdims=True)
    proj_grad = ((audio_grad - audio * along) * audio_scale).astype(jnp.bfloat16)
    half = channels // cores
    own_features = lax.dynamic_slice_in_dim(audio_features, core * half, half, 1)
    other_features = lax.dynamic_slice_in_dim(audio_features, (1 - core) * half, half, 1)
    grad_weight = summed_everywhere(
        dot(own_features, proj_grad, 0, 0), dot(other_features, proj_grad, 0, 0)
    )
    grad_features = dot(proj_grad, proj_weight, 1, 1).astype(jnp.bfloat16)
    sums = []
    for n in range(chips):
        over = SCALE * dot(tiles[chips + n], audio_b, 0, 0)
        kept = SCALE * dot(tiles[n], audio_b, 0, 0)
        sums.append(kept + shifted(over.astype(jnp.bfloat16), "core", 1))
    text_grad = sums[0]
    for n in range(1, chips):
        text_grad = text_grad + shifted(sums[n].astype(jnp.bfloat16), "zh", -n)
    text_along = jnp.sum(text * text_grad, axis=1, keepdims=True)
    grad_text = (text_grad - text * text_along) * text_scale
    return (grad_weight, grad_features, grad_text)


def solution(mesh):
    split = (4, 2, 2, 4, 8)
    fine = Mesh(mesh.devices.reshape(split), FINE)
    rows = P(FINE, None)
    return jax.shard_map(
        body,
        mesh=fine,
        in_specs=(rows, P(), rows, P(FINE)),
        out_specs=(P(), rows, rows),
        check_vma=False,
    )
```

```python
import jax
import jax.numpy as jnp
from jax import lax
from jax.experimental import pallas as pl
from jax.experimental.pallas import tpu as pltpu
from jax.sharding import Mesh, PartitionSpec as P

SCALE = 100.0
EPS = 1e-06
FINE = ("zh", "core", "zl", "x", "y")
SPLIT = (4, 2, 2, 4, 8)
PLANE = ("x", "y")
COLUMN = ("zh", "zl")
REST = 16
MIB = 1 << 20


def shifted(block, axis, distance):
    count = lax.axis_size(axis)
    return lax.ppermute(block, axis, [(i, (i + distance) % count) for i in range(count)])


def exchanged(block, axes):
    return lax.all_to_all(block, axes, split_axis=0, concat_axis=0, tiled=True)


def copies(block, count):
    return jnp.broadcast_to(block[None], (count,) + block.shape).reshape(
        (count * block.shape[0],) + block.shape[1:]
    )


def folded(block, count):
    parts = block.reshape((count, block.shape[0] // count) + block.shape[1:])
    return jnp.sum(parts.astype(jnp.float32), axis=0)


def dot(a, b, da, db):
    return lax.dot_general(a, b, (((da,), (db,)), ((), ())), preferred_element_type=jnp.float32)


def call(kernel, outs, *args, scratch=(), flops=0, limit=16):
    whole = pl.BlockSpec(memory_space=pltpu.VMEM)
    scalars = pl.BlockSpec(memory_space=pltpu.SMEM)
    size = sum(a.size * a.dtype.itemsize for a in (*args, *outs))
    return pl.pallas_call(
        kernel,
        out_shape=outs,
        in_specs=[scalars if a.shape == (2,) else whole for a in args],
        out_specs=[whole] * len(outs),
        scratch_shapes=scratch,
        compiler_params=pltpu.CompilerParams(vmem_limit_bytes=limit * MIB),
        cost_estimate=pl.CostEstimate(flops=flops, bytes_accessed=size, transcendentals=0),
    )(*args)


def shape(dims, dtype):
    return jax.ShapeDtypeStruct(dims, dtype)


def text_kernel(text_ref, main_ref, rest_ref):
    main = main_ref.shape[0]
    text = text_ref[...].astype(jnp.float32)
    scale = lax.rsqrt(jnp.sum(text * text, axis=1, keepdims=True) + EPS)
    text = (text * scale).astype(jnp.bfloat16)
    main_ref[...] = text[:main]
    rest_ref[...] = text[main:]


def audio_kernel(features_ref, weight_ref, audio_ref, audio_b_ref, scale_ref):
    proj = dot(features_ref[...], weight_ref[...], 1, 0)
    scale = lax.rsqrt(jnp.sum(proj * proj, axis=1, keepdims=True) + EPS)
    audio = proj * scale
    audio_ref[...] = audio
    audio_b_ref[...] = audio.astype(jnp.bfloat16)
    scale_ref[...] = scale


def score_kernel(
    place_ref, audio_ref, audio_b_ref, scale_ref, positive_ref, own_ref, other_ref,
    grad_ref, tiles_ref, text_ref, scores_ref,
):
    chip, core = place_ref[0], place_ref[1]
    blocks, rows, _ = tiles_ref.shape
    chips = blocks // 2
    main = rows - REST
    audio_b = audio_b_ref[...]
    for n in range(blocks):
        held = own_ref if n < chips else other_ref
        back = lax.rem(chip - n % chips + chips, chips)
        start = pl.multiple_of(chips * main + back * REST, REST)
        lane = pl.ds(n * rows, main)
        text_ref[lane, :] = held[pl.ds((n % chips) * main, main), :]
        text_ref[pl.ds(n * rows + main, REST), :] = held[pl.ds(start, REST), :]
        scores_ref[:, pl.ds(n * rows, rows)] = SCALE * dot(
            audio_b, text_ref[pl.ds(n * rows, rows), :], 1, 1
        )
    step = 16
    ids = lax.broadcasted_iota(jnp.int32, (step, rows), 1)
    for r in range(0, rows, step):
        scores = scores_ref[r : r + step, :]
        weights = jnp.exp(scores - jnp.max(scores, axis=1, keepdims=True))
        weights = weights * (1.0 / jnp.sum(weights, axis=1, keepdims=True))
        positive = positive_ref[r : r + step, :]
        for n in range(blocks):
            column = core if n < chips else 1 - core
            first = ((n % chips) * 2 + column) * rows
            match = jnp.where(positive - first == ids, 1.0, 0.0)
            part = weights[:, n * rows : (n + 1) * rows] - match
            tiles_ref[n, r : r + step, :] = part.astype(jnp.bfloat16)
    total = jnp.zeros(audio_ref.shape, jnp.float32)
    for n in range(blocks):
        total = total + dot(tiles_ref[n], text_ref[pl.ds(n * rows, rows), :], 1, 0)
    total = SCALE * total
    audio = audio_ref[...]
    along = jnp.sum(audio * total, axis=1, keepdims=True)
    grad_ref[...] = ((total - audio * along) * scale_ref[...]).astype(jnp.bfloat16)


def over_kernel(tiles_ref, audio_b_ref, over_ref):
    blocks = tiles_ref.shape[0] // 2
    for n in range(blocks):
        part = SCALE * dot(tiles_ref[blocks + n], audio_b_ref[...], 0, 0)
        over_ref[n] = part.astype(jnp.bfloat16)


def kept_kernel(place_ref, tiles_ref, audio_b_ref, over_ref, home_ref, *away_refs):
    chips = len(away_refs) + 1
    for n in range(chips):
        to = lax.rem(place_ref[0] + n, chips)
        part = SCALE * dot(tiles_ref[to], audio_b_ref[...], 0, 0)
        part = part + over_ref[to].astype(jnp.float32)
        if n == 0:
            home_ref[...] = part
        else:
            away_refs[n - 1][...] = part.astype(jnp.bfloat16)


def weight_kernel(features_ref, grad_ref, part_ref, half_ref):
    part = part_ref[...] + dot(features_ref[...], grad_ref[...], 0, 0)
    half_ref[...] = part.astype(jnp.bfloat16)


def summed_everywhere(half):
    core = lax.axis_index("core")
    plane = lax.axis_size(PLANE)
    column = lax.axis_size(COLUMN)
    part = folded(exchanged(half, PLANE), plane).astype(jnp.bfloat16)
    part = folded(exchanged(copies(part, column), COLUMN), column).astype(jnp.bfloat16)
    half = exchanged(copies(part, plane), PLANE)
    there = shifted(half, "core", 1)
    low, high = jnp.concatenate([half, there]), jnp.concatenate([there, half])
    return jnp.where(core == 0, low, high).astype(jnp.float32)


def body(audio_features, proj_weight, text_raw, positive):
    rows, channels = audio_features.shape
    width = text_raw.shape[1]
    chips = lax.axis_size("zh")
    blocks = chips * lax.axis_size("core")
    core = lax.axis_index("core")
    place = jnp.stack([lax.axis_index("zh"), core]).astype(jnp.int32)
    bf16, f32 = jnp.bfloat16, jnp.float32
    pair_flops = 2 * rows * rows * blocks * width

    main, rest = call(
        text_kernel, (shape((rows - REST, width), bf16), shape((REST, width), bf16)), text_raw
    )
    rests = [rest] + [shifted(rest, "zh", k) for k in range(1, chips)]
    main = lax.all_gather(main, "zh", axis=0, tiled=True)
    own = jnp.concatenate([main] + rests)
    own, audio_features = lax.optimization_barrier((own, audio_features))
    other = shifted(own, "core", 1)
    half = channels // 2
    features = lax.dynamic_slice_in_dim(audio_features, core * half, half, 1)
    beside = lax.dynamic_slice_in_dim(audio_features, (1 - core) * half, half, 1)
    beside = shifted(beside, "core", 1)
    audio, audio_b, scale = call(
        audio_kernel,
        (shape((rows, width), f32), shape((rows, width), bf16), shape((rows, 1), f32)),
        audio_features,
        proj_weight,
        flops=2 * rows * channels * width,
    )
    proj_grad, tiles = call(
        score_kernel,
        (shape((rows, width), bf16), shape((blocks, rows, rows), bf16)),
        place,
        audio,
        audio_b,
        scale,
        positive.reshape(rows, 1),
        own,
        other,
        scratch=[pltpu.VMEM((blocks * rows, width), bf16), pltpu.VMEM((rows, blocks * rows), f32)],
        flops=2 * pair_flops,
    )
    grad_beside = shifted(proj_grad, "core", 1)
    (weight_half,) = call(
        weight_kernel,
        (shape((half, width), bf16),),
        beside,
        grad_beside,
        dot(features, proj_grad, 0, 0),
        flops=2 * half * rows * width,
    )
    grad_weight = summed_everywhere(weight_half)
    grad_features = dot(proj_grad, proj_weight, 1, 1).astype(bf16)
    (over,) = call(
        over_kernel, (shape((chips, rows, width), bf16),), tiles, audio_b, flops=pair_flops // 2
    )
    over = shifted(over, "core", 1)
    home, *away = call(
        kept_kernel,
        (shape((rows, width), f32),) + (shape((rows, width), bf16),) * (chips - 1),
        place,
        tiles,
        audio_b,
        over,
        flops=pair_flops // 2,
    )
    text_grad = home
    for n, block in enumerate(away):
        text_grad = text_grad + shifted(block, "zh", n + 1)
    text_f = text_raw.astype(f32)
    text_scale = lax.rsqrt(jnp.sum(text_f * text_f, axis=1, keepdims=True) + EPS)
    text = text_f * text_scale
    text_along = jnp.sum(text * text_grad, axis=1, keepdims=True)
    grad_text = (text_grad - text * text_along) * text_scale
    return (grad_weight, grad_features, grad_text)


def solution(mesh):
    fine = Mesh(mesh.devices.reshape(SPLIT), FINE)
    rows = P(FINE, None)
    return jax.shard_map(
        body,
        mesh=fine,
        in_specs=(rows, P(), rows, P(FINE)),
        out_specs=(P(), rows, rows),
        check_vma=False,
    )
```

```python
import jax
import jax.numpy as jnp
from jax import lax
from jax.experimental import pallas as pl
from jax.experimental.pallas import tpu as pltpu
from jax.sharding import Mesh, PartitionSpec as P

SCALE = 100.0
EPS = 1e-06
FINE = ("zh", "core", "zl", "x", "y")
SPLIT = (4, 2, 2, 4, 8)
PLANE = ("x", "y")
COLUMN = ("zh", "zl")
MIB = 1 << 20


def shifted(block, axis, distance):
    count = lax.axis_size(axis)
    return lax.ppermute(block, axis, [(i, (i + distance) % count) for i in range(count)])


def exchanged(block, axes):
    return lax.all_to_all(block, axes, split_axis=0, concat_axis=0, tiled=True)


def dot(a, b, da, db):
    return lax.dot_general(a, b, (((da,), (db,)), ((), ())), preferred_element_type=jnp.float32)


def call(kernel, outs, *args, scratch=(), flops=0, limit=16, light=False):
    whole = pl.BlockSpec(memory_space=pltpu.VMEM)
    scalars = pl.BlockSpec(memory_space=pltpu.SMEM)
    size = 0 if light else sum(a.size * a.dtype.itemsize for a in (*args, *outs))
    return pl.pallas_call(
        kernel,
        out_shape=outs,
        in_specs=[scalars if a.shape == (2,) else whole for a in args],
        out_specs=[whole] * len(outs),
        scratch_shapes=scratch,
        compiler_params=pltpu.CompilerParams(vmem_limit_bytes=limit * MIB),
        cost_estimate=pl.CostEstimate(flops=flops, bytes_accessed=size, transcendentals=0),
    )(*args)


def shape(dims, dtype):
    return jax.ShapeDtypeStruct(dims, dtype)


def text_kernel(text_ref, copies_ref):
    text = text_ref[...].astype(jnp.float32)
    scale = lax.rsqrt(jnp.sum(text * text, axis=1, keepdims=True) + EPS)
    text = (text * scale).astype(jnp.bfloat16)
    for n in range(copies_ref.shape[0]):
        copies_ref[n] = text


def audio_kernel(features_ref, weight_ref, audio_ref, audio_b_ref, scale_ref):
    proj = dot(features_ref[...], weight_ref[...], 1, 0)
    scale = lax.rsqrt(jnp.sum(proj * proj, axis=1, keepdims=True) + EPS)
    audio = proj * scale
    audio_ref[...] = audio
    audio_b_ref[...] = audio.astype(jnp.bfloat16)
    scale_ref[...] = scale


def score_kernel(
    place_ref, audio_ref, audio_b_ref, scale_ref, positive_ref, own_ref, other_ref,
    grad_ref, tiles_ref, scores_ref,
):
    core = place_ref[1]
    blocks, rows, _ = tiles_ref.shape
    chips = blocks // 2
    audio_b = audio_b_ref[...]
    for n in range(blocks):
        text = (own_ref if n < chips else other_ref)[n % chips]
        scores_ref[:, pl.ds(n * rows, rows)] = SCALE * dot(audio_b, text, 1, 1)
    step = 16
    ids = lax.broadcasted_iota(jnp.int32, (step, rows), 1)
    for r in range(0, rows, step):
        scores = scores_ref[r : r + step, :]
        weights = jnp.exp(scores - jnp.max(scores, axis=1, keepdims=True))
        weights = weights * (1.0 / jnp.sum(weights, axis=1, keepdims=True))
        positive = positive_ref[r : r + step, :]
        for n in range(blocks):
            column = core if n < chips else 1 - core
            first = ((n % chips) * 2 + column) * rows
            match = jnp.where(positive - first == ids, 1.0, 0.0)
            part = weights[:, n * rows : (n + 1) * rows] - match
            tiles_ref[n, r : r + step, :] = part.astype(jnp.bfloat16)
    total = jnp.zeros(audio_ref.shape, jnp.float32)
    for n in range(blocks):
        text = (own_ref if n < chips else other_ref)[n % chips]
        total = total + dot(tiles_ref[n], text, 1, 0)
    total = SCALE * total
    audio = audio_ref[...]
    along = jnp.sum(audio * total, axis=1, keepdims=True)
    grad_ref[...] = ((total - audio * along) * scale_ref[...]).astype(jnp.bfloat16)


def over_kernel(tiles_ref, audio_b_ref, over_ref):
    blocks = tiles_ref.shape[0] // 2
    for n in range(blocks):
        part = SCALE * dot(tiles_ref[blocks + n], audio_b_ref[...], 0, 0)
        over_ref[n] = part.astype(jnp.bfloat16)


def kept_kernel(place_ref, tiles_ref, audio_b_ref, over_ref, home_ref, *away_refs):
    chips = len(away_refs) + 1
    for n in range(chips):
        to = lax.rem(place_ref[0] + n, chips)
        part = SCALE * dot(tiles_ref[to], audio_b_ref[...], 0, 0)
        part = part + over_ref[to].astype(jnp.float32)
        if n == 0:
            home_ref[...] = part
        else:
            away_refs[n - 1][...] = part.astype(jnp.bfloat16)


def features_kernel(grad_ref, weight_ref, out_ref):
    out_ref[...] = dot(grad_ref[...], weight_ref[...], 1, 1).astype(jnp.bfloat16)


def weight_kernel(features_ref, grad_ref, part_ref, half_ref):
    part = part_ref[...] + dot(features_ref[...], grad_ref[...], 0, 0)
    half_ref[...] = part.astype(jnp.bfloat16)


def fold_kernel(parts_ref, copies_ref):
    total = jnp.sum(parts_ref[...].astype(jnp.float32), axis=0).astype(jnp.bfloat16)
    for n in range(copies_ref.shape[0]):
        copies_ref[n] = total


def place_kernel(place_ref, half_ref, *refs):
    refs[-1][...] = half_ref[...].astype(jnp.float32)


def placed(place, half, side, whole):
    steps, (rows, width) = 4, half.shape
    tile = (rows // steps, width)
    given = [] if whole is None else [whole]
    return pl.pallas_call(
        place_kernel,
        out_shape=shape((2 * rows, width), jnp.float32),
        grid_spec=pltpu.PrefetchScalarGridSpec(
            num_scalar_prefetch=1,
            grid=(steps,),
            in_specs=[pl.BlockSpec(tile, lambda i, at: (i, 0))]
            + [pl.BlockSpec(memory_space=pl.ANY)] * len(given),
            out_specs=pl.BlockSpec(tile, lambda i, at: ((at[1] + side) % 2 * steps + i, 0)),
        ),
        input_output_aliases={2: 0} if given else {},
        compiler_params=pltpu.CompilerParams(vmem_limit_bytes=8 * MIB),
        cost_estimate=pl.CostEstimate(
            flops=0, bytes_accessed=6 * rows * width, transcendentals=0
        ),
    )(place, half, *given)


def text_grad_kernel(text_ref, home_ref, *refs):
    grad = home_ref[...]
    for ref in refs[:-1]:
        grad = grad + ref[...].astype(jnp.float32)
    text = text_ref[...].astype(jnp.float32)
    scale = lax.rsqrt(jnp.sum(text * text, axis=1, keepdims=True) + EPS)
    text = text * scale
    along = jnp.sum(text * grad, axis=1, keepdims=True)
    refs[-1][...] = (grad - text * along) * scale


def body(audio_features, proj_weight, text_raw, positive):
    rows, channels = audio_features.shape
    width = text_raw.shape[1]
    chips = lax.axis_size("zh")
    blocks = chips * lax.axis_size("core")
    core = lax.axis_index("core")
    place = jnp.stack([lax.axis_index("zh"), core]).astype(jnp.int32)
    bf16, f32 = jnp.bfloat16, jnp.float32
    pair_flops = 2 * rows * rows * blocks * width

    (text_b,) = call(text_kernel, (shape((chips, rows, width), bf16),), text_raw)
    own = exchanged(text_b, "zh")
    other = shifted(own, "core", 1)
    half = channels // 2
    features = lax.dynamic_slice_in_dim(audio_features, core * half, half, 1)
    beside = lax.dynamic_slice_in_dim(audio_features, (1 - core) * half, half, 1)
    beside = shifted(beside, "core", 1)
    audio, audio_b, scale = call(
        audio_kernel,
        (shape((rows, width), f32), shape((rows, width), bf16), shape((rows, 1), f32)),
        audio_features,
        proj_weight,
        flops=2 * rows * channels * width,
    )
    proj_grad, tiles = call(
        score_kernel,
        (shape((rows, width), bf16), shape((blocks, rows, rows), bf16)),
        place,
        audio,
        audio_b,
        scale,
        positive.reshape(rows, 1),
        own,
        other,
        scratch=[pltpu.VMEM((rows, blocks * rows), f32)],
        flops=2 * pair_flops,
    )
    grad_beside = shifted(proj_grad, "core", 1)
    (weight_half,) = call(
        weight_kernel,
        (shape((half, width), bf16),),
        beside,
        grad_beside,
        dot(features, proj_grad, 0, 0),
        flops=2 * half * rows * width,
    )
    weight_half, tiles = lax.optimization_barrier((weight_half, tiles))
    plane = lax.axis_size(PLANE)
    column = lax.axis_size(COLUMN)
    part = half // plane
    parts = exchanged(weight_half.reshape(plane, part, width), PLANE)
    (grad_features,) = call(
        features_kernel,
        (shape((rows, channels), bf16),),
        proj_grad,
        proj_weight,
        flops=40 * rows * channels * width,
    )
    grad_features, tiles = lax.optimization_barrier((grad_features, tiles))
    (over,) = call(
        over_kernel, (shape((chips, rows, width), bf16),), tiles, audio_b, light=True
    )
    over = shifted(over, "core", 1)
    home, *away = call(
        kept_kernel,
        (shape((rows, width), f32),) + (shape((rows, width), bf16),) * (chips - 1),
        place,
        tiles,
        audio_b,
        over,
        light=True,
    )
    parts, home, away, grad_features = lax.optimization_barrier(
        (parts, home, away, grad_features)
    )
    (parts,) = call(fold_kernel, (shape((column, part, width), bf16),), parts)
    parts = exchanged(parts, COLUMN)
    away = [shifted(block, "zh", n + 1) for n, block in enumerate(away)]
    (parts,) = call(fold_kernel, (shape((plane, part, width), bf16),), parts)
    weight_half = exchanged(parts, PLANE).reshape(half, width)
    weight_half, away = lax.optimization_barrier((weight_half, away))
    there = shifted(weight_half, "core", 1)
    grad_weight = placed(place, weight_half, 0, None)
    grad_weight = placed(place, there, 1, grad_weight)
    (grad_text,) = call(text_grad_kernel, (shape((rows, width), f32),), text_raw, home, *away)
    return (grad_weight, grad_features, grad_text)


def solution(mesh):
    fine = Mesh(mesh.devices.reshape(SPLIT), FINE)
    rows = P(FINE, None)
    return jax.shard_map(
        body,
        mesh=fine,
        in_specs=(rows, P(), rows, P(FINE)),
        out_specs=(P(), rows, rows),
        check_vma=False,
    )
```

```python
import jax
import jax.numpy as jnp
from jax import lax
from jax.experimental import pallas as pl
from jax.experimental.pallas import tpu as pltpu
from jax.sharding import Mesh, PartitionSpec as P

SCALE = 100.0
EPS = 1e-06
FINE = ("zh", "core", "zl", "x", "y")
SPLIT = (4, 2, 2, 4, 8)
PLANE = ("x", "y")
COLUMN = ("zh", "zl")
TAIL = 16
MIB = 1 << 20


def shifted(block, axis, distance):
    count = lax.axis_size(axis)
    return lax.ppermute(block, axis, [(i, (i + distance) % count) for i in range(count)])


def exchanged(block, axes):
    return lax.all_to_all(block, axes, split_axis=0, concat_axis=0, tiled=True)


def dot(a, b, da, db):
    return lax.dot_general(a, b, (((da,), (db,)), ((), ())), preferred_element_type=jnp.float32)


def call(kernel, outs, *args, scratch=(), flops=0, limit=16, light=False):
    whole = pl.BlockSpec(memory_space=pltpu.VMEM)
    scalars = pl.BlockSpec(memory_space=pltpu.SMEM)
    size = 0 if light else sum(a.size * a.dtype.itemsize for a in (*args, *outs))
    return pl.pallas_call(
        kernel,
        out_shape=outs,
        in_specs=[scalars if a.shape == (2,) else whole for a in args],
        out_specs=[whole] * len(outs),
        scratch_shapes=scratch,
        compiler_params=pltpu.CompilerParams(vmem_limit_bytes=limit * MIB),
        cost_estimate=pl.CostEstimate(flops=flops, bytes_accessed=size, transcendentals=0),
    )(*args)


def shape(dims, dtype):
    return jax.ShapeDtypeStruct(dims, dtype)


def text_kernel(text_ref, sent_ref):
    rows = text_ref.shape[0]
    text = text_ref[...].astype(jnp.float32)
    scale = lax.rsqrt(jnp.sum(text * text, axis=1, keepdims=True) + EPS)
    text = (text * scale).astype(jnp.bfloat16).astype(jnp.float32)
    largest = jnp.max(jnp.max(jnp.abs(text), axis=1, keepdims=True), axis=0, keepdims=True)
    power = jnp.floor(jnp.log2(jnp.maximum(largest, 1e-30))) - 13.0
    sent_ref[:rows, :] = (text * jnp.exp2(-power)).astype(jnp.bfloat16)
    tail = (sent_ref.shape[0] - rows, sent_ref.shape[1])
    sent_ref[rows:, :] = jnp.broadcast_to(power, tail).astype(jnp.bfloat16)


def audio_kernel(features_ref, weight_ref, audio_ref, audio_b_ref, scale_ref):
    proj = dot(features_ref[...], weight_ref[...], 1, 0)
    scale = lax.rsqrt(jnp.sum(proj * proj, axis=1, keepdims=True) + EPS)
    audio = proj * scale
    audio_ref[...] = audio
    audio_b_ref[...] = audio.astype(jnp.bfloat16)
    scale_ref[...] = scale


def score_kernel(
    place_ref, audio_ref, audio_b_ref, scale_ref, features_ref, positive_ref, own_ref, other_ref,
    grad_ref, tiles_ref, sent_ref, scores_ref,
):
    core = place_ref[1]
    blocks, rows, _ = tiles_ref.shape
    chips = blocks // 2
    audio_b = audio_b_ref[...]

    def text(n):
        held = own_ref if n < chips else other_ref
        start = n % chips * (rows + TAIL)
        power = held[start + rows : start + rows + TAIL, :128].astype(jnp.float32)
        return held[start : start + rows, :], SCALE * jnp.exp2(power[:1, :1])

    for n in range(blocks):
        block, scale = text(n)
        scores_ref[:, n * rows : (n + 1) * rows] = scale * dot(audio_b, block, 1, 1)
    step = 16
    ids = lax.broadcasted_iota(jnp.int32, (step, rows), 1)
    for r in range(0, rows, step):
        scores = scores_ref[r : r + step, :]
        weights = jnp.exp(scores - jnp.max(scores, axis=1, keepdims=True))
        weights = weights * (1.0 / jnp.sum(weights, axis=1, keepdims=True))
        positive = positive_ref[r : r + step, :]
        for n in range(blocks):
            column = core if n < chips else 1 - core
            first = ((n % chips) * 2 + column) * rows
            match = jnp.where(positive - first == ids, 1.0, 0.0)
            part = weights[:, n * rows : (n + 1) * rows] - match
            tiles_ref[n, r : r + step, :] = part.astype(jnp.bfloat16)
    total = jnp.zeros(audio_ref.shape, jnp.float32)
    for n in range(blocks):
        block, scale = text(n)
        total = total + scale * dot(tiles_ref[n], block, 1, 0)
    audio = audio_ref[...]
    along = jnp.sum(audio * total, axis=1, keepdims=True)
    grad = ((total - audio * along) * scale_ref[...]).astype(jnp.bfloat16)
    grad_ref[...] = grad
    half = features_ref.shape[1] // 2
    features = features_ref[:, pl.ds(pl.multiple_of((1 - core) * half, half), half)]
    sent_ref[:half, :] = dot(features, grad, 0, 0).astype(jnp.bfloat16)
    for n in range(chips):
        part = SCALE * dot(tiles_ref[chips + n], audio_b, 0, 0)
        sent_ref[half + n * rows : half + (n + 1) * rows, :] = part.astype(jnp.bfloat16)


def own_kernel(place_ref, features_ref, grad_ref, weight_ref):
    half = features_ref.shape[1] // 2
    features = features_ref[:, pl.ds(pl.multiple_of(place_ref[1] * half, half), half)]
    weight_ref[...] = dot(features, grad_ref[...], 0, 0)


def half_kernel(weight_ref, got_ref, half_ref):
    parts, rows, width = half_ref.shape
    total = weight_ref[...] + got_ref[: parts * rows, :].astype(jnp.float32)
    half_ref[...] = total.astype(jnp.bfloat16).reshape(parts, rows, width)


def features_kernel(grad_ref, weight_ref, out_ref):
    out_ref[...] = dot(grad_ref[...], weight_ref[...], 1, 1).astype(jnp.bfloat16)


def text_sums_kernel(
    place_ref, tiles_ref, audio_b_ref, got_ref,
    home_ref, next_ref, last_ref, forward_ref, backward_ref,
):
    rows = home_ref.shape[0]
    chips = tiles_ref.shape[0] // 2
    half = got_ref.shape[0] - chips * rows

    def sums(distance):
        to = lax.rem(place_ref[0] + distance, chips)
        start = pl.multiple_of(half + to * rows, rows)
        part = SCALE * dot(tiles_ref[to], audio_b_ref[...], 0, 0)
        return part + got_ref[pl.ds(start, rows), :].astype(jnp.float32)

    home_ref[...] = sums(0)
    next_ref[...] = sums(1)
    last_ref[...] = sums(chips - 1)
    across = sums(2).astype(jnp.bfloat16)
    forward_ref[...] = across[: rows // 2]
    backward_ref[...] = across[rows // 2 :]


def relay_kernel(next_ref, last_ref, forward_ref, backward_ref, to_next_ref, to_last_ref):
    cut = next_ref.shape[0] // 2
    ahead = next_ref[:cut, :] + forward_ref[...].astype(jnp.float32)
    behind = last_ref[cut:, :] + backward_ref[...].astype(jnp.float32)
    to_next_ref[:cut, :] = ahead.astype(jnp.bfloat16)
    to_next_ref[cut:, :] = next_ref[cut:, :].astype(jnp.bfloat16)
    to_last_ref[:cut, :] = last_ref[:cut, :].astype(jnp.bfloat16)
    to_last_ref[cut:, :] = behind.astype(jnp.bfloat16)


def fold_kernel(parts_ref, copies_ref):
    total = jnp.sum(parts_ref[...].astype(jnp.float32), axis=0).astype(jnp.bfloat16)
    for n in range(copies_ref.shape[0]):
        copies_ref[n] = total


def place_kernel(place_ref, half_ref, *refs):
    refs[-1][...] = half_ref[...].astype(jnp.float32)


def placed(place, half, side, whole):
    rows, width = half.shape
    given = [] if whole is None else [whole]
    return pl.pallas_call(
        place_kernel,
        out_shape=shape((2 * rows, width), jnp.float32),
        grid_spec=pltpu.PrefetchScalarGridSpec(
            num_scalar_prefetch=1,
            grid=(1,),
            in_specs=[pl.BlockSpec((rows, width), lambda i, at: (0, 0))]
            + [pl.BlockSpec(memory_space=pl.ANY)] * len(given),
            out_specs=pl.BlockSpec((rows, width), lambda i, at: ((at[1] + side) % 2, 0)),
        ),
        input_output_aliases={2: 0} if given else {},
        compiler_params=pltpu.CompilerParams(vmem_limit_bytes=8 * MIB),
        cost_estimate=pl.CostEstimate(
            flops=0, bytes_accessed=6 * rows * width, transcendentals=0
        ),
    )(place, half, *given)


def text_grad_kernel(text_ref, home_ref, *refs):
    grad = home_ref[...]
    for ref in refs[:-1]:
        grad = grad + ref[...].astype(jnp.float32)
    text = text_ref[...].astype(jnp.float32)
    scale = lax.rsqrt(jnp.sum(text * text, axis=1, keepdims=True) + EPS)
    text = text * scale
    along = jnp.sum(text * grad, axis=1, keepdims=True)
    refs[-1][...] = (grad - text * along) * scale


def body(audio_features, proj_weight, text_raw, positive):
    rows, channels = audio_features.shape
    width = text_raw.shape[1]
    chips = lax.axis_size("zh")
    blocks = chips * lax.axis_size("core")
    place = jnp.stack([lax.axis_index("zh"), lax.axis_index("core")]).astype(jnp.int32)
    bf16, f32 = jnp.bfloat16, jnp.float32
    pair_flops = 2 * rows * rows * blocks * width
    half = channels // 2
    block = shape((rows, width), f32)
    block_b = shape((rows, width), bf16)
    cut_b = shape((rows // 2, width), bf16)

    (sent,) = call(text_kernel, (shape((rows + TAIL, width), bf16),), text_raw)
    own = lax.all_gather(sent.astype(jnp.float16), "zh", axis=0, tiled=True).astype(bf16)
    own, audio_features = lax.optimization_barrier((own, audio_features))
    other = shifted(own, "core", 1)
    audio, audio_b, scale = call(
        audio_kernel,
        (block, block_b, shape((rows, 1), f32)),
        audio_features,
        proj_weight,
        flops=2 * rows * channels * width,
    )
    proj_grad, tiles, sent = call(
        score_kernel,
        (block_b, shape((blocks, rows, rows), bf16), shape((half + chips * rows, width), bf16)),
        place,
        audio,
        audio_b,
        scale,
        audio_features,
        positive.reshape(rows, 1),
        own,
        other,
        scratch=[pltpu.VMEM((rows, blocks * rows), f32)],
        flops=3 * pair_flops,
        limit=20,
    )
    got = shifted(sent, "core", 1)
    (weight,) = call(
        own_kernel, (shape((half, width), f32),), place, audio_features, proj_grad, light=True
    )
    (grad_features,) = call(
        features_kernel, (shape((rows, channels), bf16),), proj_grad, proj_weight, light=True
    )
    got, weight, grad_features = lax.optimization_barrier((got, weight, grad_features))
    plane = lax.axis_size(PLANE)
    column = lax.axis_size(COLUMN)
    part = half // plane
    (parts,) = call(half_kernel, (shape((plane, part, width), bf16),), weight, got)
    parts, got = lax.optimization_barrier((parts, got))
    parts = exchanged(parts, PLANE)
    home, following, last, forward, backward = call(
        text_sums_kernel,
        (block, block, block, cut_b, cut_b),
        place,
        tiles,
        audio_b,
        got,
        flops=pair_flops,
    )
    forward = shifted(forward, "zh", 1)
    backward = shifted(backward, "zh", -1)
    parts, forward, backward = lax.optimization_barrier((parts, forward, backward))
    (parts,) = call(fold_kernel, (shape((column, part, width), bf16),), parts)
    parts = exchanged(parts, COLUMN)
    to_next, to_last = call(
        relay_kernel, (block_b, block_b), following, last, forward, backward, light=True
    )
    (parts,) = call(fold_kernel, (shape((plane, part, width), bf16),), parts)
    parts, to_next, to_last = lax.optimization_barrier((parts, to_next, to_last))
    weight_half = exchanged(parts, PLANE).reshape(half, width)
    arrived = [shifted(to_next, "zh", 1), shifted(to_last, "zh", -1)]
    weight_half, arrived = lax.optimization_barrier((weight_half, arrived))
    there = shifted(weight_half, "core", 1)
    grad_weight = placed(place, weight_half, 0, None)
    grad_weight = placed(place, there, 1, grad_weight)
    (grad_text,) = call(text_grad_kernel, (block,), text_raw, home, *arrived)
    return (grad_weight, grad_features, grad_text)


def solution(mesh):
    fine = Mesh(mesh.devices.reshape(SPLIT), FINE)
    rows = P(FINE, None)
    return jax.shard_map(
        body,
        mesh=fine,
        in_specs=(rows, P(), rows, P(FINE)),
        out_specs=(P(), rows, rows),
        check_vma=False,
    )
```

```python
import jax
import jax.numpy as jnp
from jax import lax
from jax.experimental import pallas as pl
from jax.experimental.pallas import tpu as pltpu
from jax.sharding import Mesh, PartitionSpec as P

SCALE = 100.0
EPS = 1e-06
FINE = ("zh", "core", "zl", "x", "y")
SPLIT = (4, 2, 2, 4, 8)
PLANE = ("x", "y")
COLUMN = ("zh", "zl")
TAIL = 16
MIB = 1 << 20


def shifted(block, axis, distance):
    count = lax.axis_size(axis)
    return lax.ppermute(block, axis, [(i, (i + distance) % count) for i in range(count)])


def exchanged(block, axes):
    return lax.all_to_all(block, axes, split_axis=0, concat_axis=0, tiled=True)


def dot(a, b, da, db):
    return lax.dot_general(a, b, (((da,), (db,)), ((), ())), preferred_element_type=jnp.float32)


def call(kernel, outs, *args, scratch=(), flops=0, limit=16, light=False):
    whole = pl.BlockSpec(memory_space=pltpu.VMEM)
    scalars = pl.BlockSpec(memory_space=pltpu.SMEM)
    size = 0 if light else sum(a.size * a.dtype.itemsize for a in (*args, *outs))
    return pl.pallas_call(
        kernel,
        out_shape=outs,
        in_specs=[scalars if a.shape == (2,) else whole for a in args],
        out_specs=[whole] * len(outs),
        scratch_shapes=scratch,
        compiler_params=pltpu.CompilerParams(vmem_limit_bytes=limit * MIB),
        cost_estimate=pl.CostEstimate(flops=flops, bytes_accessed=size, transcendentals=0),
    )(*args)


def shape(dims, dtype):
    return jax.ShapeDtypeStruct(dims, dtype)


def text_kernel(text_ref, sent_ref):
    rows = text_ref.shape[0]
    text = text_ref[...].astype(jnp.float32)
    scale = lax.rsqrt(jnp.sum(text * text, axis=1, keepdims=True) + EPS)
    text = (text * scale).astype(jnp.bfloat16).astype(jnp.float32)
    largest = jnp.max(jnp.max(jnp.abs(text), axis=1, keepdims=True), axis=0, keepdims=True)
    power = jnp.floor(jnp.log2(jnp.maximum(largest, 1e-30))) - 13.0
    sent_ref[:rows, :] = (text * jnp.exp2(-power)).astype(jnp.bfloat16)
    tail = (sent_ref.shape[0] - rows, sent_ref.shape[1])
    sent_ref[rows:, :] = jnp.broadcast_to(power, tail).astype(jnp.bfloat16)


def audio_kernel(features_ref, weight_ref, audio_ref, audio_b_ref, scale_ref):
    proj = dot(features_ref[...], weight_ref[...], 1, 0)
    scale = lax.rsqrt(jnp.sum(proj * proj, axis=1, keepdims=True) + EPS)
    audio = proj * scale
    audio_ref[...] = audio
    audio_b_ref[...] = audio.astype(jnp.bfloat16)
    scale_ref[...] = scale


def score_kernel(
    place_ref, audio_ref, audio_b_ref, scale_ref, features_ref, positive_ref, own_ref, other_ref,
    grad_ref, tiles_ref, sent_ref, scores_ref,
):
    core = place_ref[1]
    blocks, rows, _ = tiles_ref.shape
    chips = blocks // 2
    audio_b = audio_b_ref[...]

    def text(n):
        held = own_ref if n < chips else other_ref
        start = n % chips * (rows + TAIL)
        power = held[start + rows : start + rows + TAIL, :128].astype(jnp.float32)
        return held[start : start + rows, :], SCALE * jnp.exp2(power[:1, :1])

    for n in range(blocks):
        block, scale = text(n)
        scores_ref[:, n * rows : (n + 1) * rows] = scale * dot(audio_b, block, 1, 1)
    step = 16
    ids = lax.broadcasted_iota(jnp.int32, (step, rows), 1)
    for r in range(0, rows, step):
        scores = scores_ref[r : r + step, :]
        weights = jnp.exp(scores - jnp.max(scores, axis=1, keepdims=True))
        weights = weights * (1.0 / jnp.sum(weights, axis=1, keepdims=True))
        positive = positive_ref[r : r + step, :]
        for n in range(blocks):
            column = core if n < chips else 1 - core
            first = ((n % chips) * 2 + column) * rows
            match = jnp.where(positive - first == ids, 1.0, 0.0)
            part = weights[:, n * rows : (n + 1) * rows] - match
            tiles_ref[n, r : r + step, :] = part.astype(jnp.bfloat16)
    total = jnp.zeros(audio_ref.shape, jnp.float32)
    for n in range(blocks):
        block, scale = text(n)
        total = total + scale * dot(tiles_ref[n], block, 1, 0)
    audio = audio_ref[...]
    along = jnp.sum(audio * total, axis=1, keepdims=True)
    grad = ((total - audio * along) * scale_ref[...]).astype(jnp.bfloat16)
    grad_ref[...] = grad
    half = features_ref.shape[1] // 2
    features = features_ref[:, pl.ds(pl.multiple_of((1 - core) * half, half), half)]
    sent_ref[:half, :] = dot(features, grad, 0, 0).astype(jnp.bfloat16)
    for n in range(chips):
        part = SCALE * dot(tiles_ref[chips + n], audio_b, 0, 0)
        sent_ref[half + n * rows : half + (n + 1) * rows, :] = part.astype(jnp.bfloat16)


def own_kernel(place_ref, features_ref, grad_ref, weight_ref):
    half = features_ref.shape[1] // 2
    features = features_ref[:, pl.ds(pl.multiple_of(place_ref[1] * half, half), half)]
    weight_ref[...] = dot(features, grad_ref[...], 0, 0)


def half_kernel(weight_ref, got_ref, half_ref):
    parts, rows, width = half_ref.shape
    total = weight_ref[...] + got_ref[: parts * rows, :].astype(jnp.float32)
    half_ref[...] = total.astype(jnp.bfloat16).reshape(parts, rows, width)


def features_kernel(grad_ref, weight_ref, out_ref):
    out_ref[...] = dot(grad_ref[...], weight_ref[...], 1, 1).astype(jnp.bfloat16)


def text_sums_kernel(tiles_ref, audio_b_ref, got_ref, sums_ref):
    chips = tiles_ref.shape[0] // 2
    rows = sums_ref.shape[0] // chips
    half = got_ref.shape[0] - chips * rows
    for n in range(chips):
        part = SCALE * dot(tiles_ref[n], audio_b_ref[...], 0, 0)
        part = part + got_ref[half + n * rows : half + (n + 1) * rows, :].astype(jnp.float32)
        sums_ref[n * rows : (n + 1) * rows, :] = part.astype(jnp.bfloat16)


def fold_kernel(parts_ref, copies_ref):
    total = jnp.sum(parts_ref[...].astype(jnp.float32), axis=0).astype(jnp.bfloat16)
    for n in range(copies_ref.shape[0]):
        copies_ref[n] = total


def place_kernel(place_ref, half_ref, *refs):
    refs[-1][...] = half_ref[...].astype(jnp.float32)


def placed(place, half, side, whole):
    rows, width = half.shape
    given = [] if whole is None else [whole]
    return pl.pallas_call(
        place_kernel,
        out_shape=shape((2 * rows, width), jnp.float32),
        grid_spec=pltpu.PrefetchScalarGridSpec(
            num_scalar_prefetch=1,
            grid=(1,),
            in_specs=[pl.BlockSpec((rows, width), lambda i, at: (0, 0))]
            + [pl.BlockSpec(memory_space=pl.ANY)] * len(given),
            out_specs=pl.BlockSpec((rows, width), lambda i, at: ((at[1] + side) % 2, 0)),
        ),
        input_output_aliases={2: 0} if given else {},
        compiler_params=pltpu.CompilerParams(vmem_limit_bytes=8 * MIB),
        cost_estimate=pl.CostEstimate(
            flops=0, bytes_accessed=6 * rows * width, transcendentals=0
        ),
    )(place, half, *given)


def text_grad_kernel(text_ref, sum_ref, grad_ref):
    grad = sum_ref[...].astype(jnp.float32)
    text = text_ref[...].astype(jnp.float32)
    scale = lax.rsqrt(jnp.sum(text * text, axis=1, keepdims=True) + EPS)
    text = text * scale
    along = jnp.sum(text * grad, axis=1, keepdims=True)
    grad_ref[...] = (grad - text * along) * scale


def body(audio_features, proj_weight, text_raw, positive):
    rows, channels = audio_features.shape
    width = text_raw.shape[1]
    chips = lax.axis_size("zh")
    blocks = chips * lax.axis_size("core")
    place = jnp.stack([lax.axis_index("zh"), lax.axis_index("core")]).astype(jnp.int32)
    bf16, f32 = jnp.bfloat16, jnp.float32
    pair_flops = 2 * rows * rows * blocks * width
    half = channels // 2
    block = shape((rows, width), f32)
    block_b = shape((rows, width), bf16)

    (sent,) = call(text_kernel, (shape((rows + TAIL, width), bf16),), text_raw)
    own = lax.all_gather(sent.astype(jnp.float16), "zh", axis=0, tiled=True).astype(bf16)
    own, audio_features = lax.optimization_barrier((own, audio_features))
    other = shifted(own, "core", 1)
    audio, audio_b, scale = call(
        audio_kernel,
        (block, block_b, shape((rows, 1), f32)),
        audio_features,
        proj_weight,
        flops=2 * rows * channels * width,
    )
    proj_grad, tiles, sent = call(
        score_kernel,
        (block_b, shape((blocks, rows, rows), bf16), shape((half + chips * rows, width), bf16)),
        place,
        audio,
        audio_b,
        scale,
        audio_features,
        positive.reshape(rows, 1),
        own,
        other,
        scratch=[pltpu.VMEM((rows, blocks * rows), f32)],
        flops=3 * pair_flops,
        limit=20,
    )
    got = shifted(sent, "core", 1)
    (weight,) = call(
        own_kernel, (shape((half, width), f32),), place, audio_features, proj_grad, light=True
    )
    (grad_features,) = call(
        features_kernel, (shape((rows, channels), bf16),), proj_grad, proj_weight, light=True
    )
    got, weight, grad_features = lax.optimization_barrier((got, weight, grad_features))
    plane = lax.axis_size(PLANE)
    column = lax.axis_size(COLUMN)
    part = half // plane
    (parts,) = call(half_kernel, (shape((plane, part, width), bf16),), weight, got)
    parts, got = lax.optimization_barrier((parts, got))
    parts = exchanged(parts, PLANE)
    (sums,) = call(
        text_sums_kernel, (shape((chips * rows, width), bf16),), tiles, audio_b, got, light=True
    )
    text_grad = lax.psum_scatter(sums, "zh", scatter_dimension=0, tiled=True)
    (parts,) = call(fold_kernel, (shape((column, part, width), bf16),), parts)
    parts = exchanged(parts, COLUMN)
    (parts,) = call(fold_kernel, (shape((plane, part, width), bf16),), parts)
    weight_half = exchanged(parts, PLANE).reshape(half, width)
    there = shifted(weight_half, "core", 1)
    grad_weight = placed(place, weight_half, 0, None)
    grad_weight = placed(place, there, 1, grad_weight)
    (grad_text,) = call(text_grad_kernel, (block,), text_raw, text_grad)
    return (grad_weight, grad_features, grad_text)


def solution(mesh):
    fine = Mesh(mesh.devices.reshape(SPLIT), FINE)
    rows = P(FINE, None)
    return jax.shard_map(
        body,
        mesh=fine,
        in_specs=(rows, P(), rows, P(FINE)),
        out_specs=(P(), rows, rows),
        check_vma=False,
    )
```

```python
import jax
import jax.numpy as jnp
from jax import lax
from jax.experimental import pallas as pl
from jax.experimental.pallas import tpu as pltpu
from jax.sharding import Mesh, PartitionSpec as P

SCALE = 100.0
EPS = 1e-06
FINE = ("zh", "core", "zl", "x", "y")
SPLIT = (4, 2, 2, 4, 8)
PLANE = ("x", "y")
COLUMN = ("zh", "zl")
TAIL = 16
MIB = 1 << 20


def shifted(block, axis, distance):
    count = lax.axis_size(axis)
    return lax.ppermute(block, axis, [(i, (i + distance) % count) for i in range(count)])


def exchanged(block, axes):
    return lax.all_to_all(block, axes, split_axis=0, concat_axis=0, tiled=True)


def dot(a, b, da, db):
    return lax.dot_general(a, b, (((da,), (db,)), ((), ())), preferred_element_type=jnp.float32)


def call(kernel, outs, *args, scratch=(), flops=0, limit=16, light=False, far=(), far_outs=False):
    whole = pl.BlockSpec(memory_space=pltpu.VMEM)
    scalars = pl.BlockSpec(memory_space=pltpu.SMEM)
    hbm = pl.BlockSpec(memory_space=pltpu.HBM)
    size = 0 if light else sum(a.size * a.dtype.itemsize for a in (*args, *outs))
    args = [
        pltpu.with_memory_space_constraint(a, pltpu.HBM) if n in far else a
        for n, a in enumerate(args)
    ]
    staged = [args[n] for n in far] + (list(outs) if far_outs else [])

    def staging(*refs):
        refs = list(refs)
        sems = refs.pop() if staged else None
        count = len(refs) - len(staged)
        refs, buffers = refs[:count], refs[count:]
        moves = []
        for n, at in enumerate(far):
            moves.append(pltpu.make_async_copy(refs[at], buffers[n], sems.at[n]))
            refs[at] = buffers[n]
        for move in moves:
            move.start()
        for move in moves:
            move.wait()
        moves = []
        if far_outs:
            for n in range(len(far), len(staged)):
                at = len(args) + n - len(far)
                moves.append(pltpu.make_async_copy(buffers[n], refs[at], sems.at[n]))
                refs[at] = buffers[n]
        kernel(*refs)
        for move in moves:
            move.start()
        for move in moves:
            move.wait()

    buffers = [pltpu.VMEM(a.shape, a.dtype) for a in staged]
    if staged:
        buffers.append(pltpu.SemaphoreType.DMA((len(staged),)))
    return pl.pallas_call(
        staging,
        out_shape=[pltpu.HBM(a.shape, a.dtype) for a in outs] if far_outs else outs,
        in_specs=[
            scalars if a.shape == (2,) else hbm if n in far else whole for n, a in enumerate(args)
        ],
        out_specs=[hbm if far_outs else whole] * len(outs),
        scratch_shapes=[*scratch, *buffers],
        compiler_params=pltpu.CompilerParams(vmem_limit_bytes=limit * MIB),
        cost_estimate=pl.CostEstimate(flops=flops, bytes_accessed=size, transcendentals=0),
    )(*args)


def shape(dims, dtype):
    return jax.ShapeDtypeStruct(dims, dtype)


def text_kernel(text_ref, sent_ref):
    rows = text_ref.shape[0]
    text = text_ref[...].astype(jnp.float32)
    scale = lax.rsqrt(jnp.sum(text * text, axis=1, keepdims=True) + EPS)
    text = (text * scale).astype(jnp.bfloat16).astype(jnp.float32)
    largest = jnp.max(jnp.max(jnp.abs(text), axis=1, keepdims=True), axis=0, keepdims=True)
    power = jnp.floor(jnp.log2(jnp.maximum(largest, 1e-30))) - 13.0
    sent_ref[:rows, :] = (text * jnp.exp2(-power)).astype(jnp.bfloat16)
    tail = (sent_ref.shape[0] - rows, sent_ref.shape[1])
    sent_ref[rows:, :] = jnp.broadcast_to(power, tail).astype(jnp.bfloat16)


def audio_kernel(features_ref, weight_ref, audio_ref, audio_b_ref, scale_ref):
    proj = dot(features_ref[...], weight_ref[...], 1, 0)
    scale = lax.rsqrt(jnp.sum(proj * proj, axis=1, keepdims=True) + EPS)
    audio = proj * scale
    audio_ref[...] = audio
    audio_b_ref[...] = audio.astype(jnp.bfloat16)
    scale_ref[...] = scale


def score_kernel(
    place_ref, audio_ref, audio_b_ref, scale_ref, features_ref, positive_ref, own_ref, other_ref,
    grad_ref, tiles_ref, sent_ref, scores_ref,
):
    core = place_ref[1]
    blocks, rows, _ = tiles_ref.shape
    chips = blocks // 2
    audio_b = audio_b_ref[...]

    def text(n):
        held = own_ref if n < chips else other_ref
        start = n % chips * (rows + TAIL)
        power = held[start + rows : start + rows + TAIL, :128].astype(jnp.float32)
        return held[start : start + rows, :], SCALE * jnp.exp2(power[:1, :1])

    for n in range(blocks):
        block, scale = text(n)
        scores_ref[:, n * rows : (n + 1) * rows] = scale * dot(audio_b, block, 1, 1)
    step = 16
    ids = lax.broadcasted_iota(jnp.int32, (step, rows), 1)
    for r in range(0, rows, step):
        scores = scores_ref[r : r + step, :]
        weights = jnp.exp(scores - jnp.max(scores, axis=1, keepdims=True))
        weights = weights * (1.0 / jnp.sum(weights, axis=1, keepdims=True))
        positive = positive_ref[r : r + step, :]
        for n in range(blocks):
            column = core if n < chips else 1 - core
            first = ((n % chips) * 2 + column) * rows
            match = jnp.where(positive - first == ids, 1.0, 0.0)
            part = weights[:, n * rows : (n + 1) * rows] - match
            tiles_ref[n, r : r + step, :] = part.astype(jnp.bfloat16)
    total = jnp.zeros(audio_ref.shape, jnp.float32)
    for n in range(blocks):
        block, scale = text(n)
        total = total + scale * dot(tiles_ref[n], block, 1, 0)
    audio = audio_ref[...]
    along = jnp.sum(audio * total, axis=1, keepdims=True)
    grad = ((total - audio * along) * scale_ref[...]).astype(jnp.bfloat16)
    grad_ref[...] = grad
    half = features_ref.shape[1] // 2
    features = features_ref[:, pl.ds(pl.multiple_of((1 - core) * half, half), half)]
    sent_ref[:half, :] = dot(features, grad, 0, 0).astype(jnp.bfloat16)
    for n in range(chips):
        part = SCALE * dot(tiles_ref[chips + n], audio_b, 0, 0)
        sent_ref[half + n * rows : half + (n + 1) * rows, :] = part.astype(jnp.bfloat16)


def own_kernel(place_ref, features_ref, grad_ref, weight_ref):
    half = features_ref.shape[1] // 2
    features = features_ref[:, pl.ds(pl.multiple_of(place_ref[1] * half, half), half)]
    weight_ref[...] = dot(features, grad_ref[...], 0, 0)


def half_kernel(weight_ref, got_ref, half_ref):
    parts, rows, width = half_ref.shape
    total = weight_ref[...] + got_ref[: parts * rows, :].astype(jnp.float32)
    half_ref[...] = total.astype(jnp.bfloat16).reshape(parts, rows, width)


def features_kernel(grad_ref, weight_ref, out_ref):
    out_ref[...] = dot(grad_ref[...], weight_ref[...], 1, 1).astype(jnp.bfloat16)


def summed(place_ref, tiles_ref, audio_b_ref, got_ref, distance):
    chips, rows = tiles_ref.shape[0] // 2, tiles_ref.shape[2]
    to = lax.rem(place_ref[0] + distance, chips)
    start = pl.multiple_of(got_ref.shape[0] - chips * rows + to * rows, rows)
    part = SCALE * dot(tiles_ref[to], audio_b_ref[...], 0, 0)
    return part + got_ref[pl.ds(start, rows), :].astype(jnp.float32)


def text_sums_kernel(place_ref, tiles_ref, audio_b_ref, got_ref, across_ref, last_ref):
    refs = (place_ref, tiles_ref, audio_b_ref, got_ref)
    across_ref[...] = summed(*refs, 2).astype(jnp.bfloat16)
    last_ref[...] = summed(*refs, 3).astype(jnp.bfloat16)


def relay_kernel(
    place_ref, tiles_ref, audio_b_ref, got_ref, across_ref, last_ref, to_next_ref, home_ref
):
    refs = (place_ref, tiles_ref, audio_b_ref, got_ref)
    ahead = summed(*refs, 1) + across_ref[...].astype(jnp.float32)
    to_next_ref[...] = ahead.astype(jnp.bfloat16)
    home_ref[...] = summed(*refs, 0) + last_ref[...].astype(jnp.float32)


def fold_kernel(parts_ref, copies_ref):
    total = jnp.sum(parts_ref[...].astype(jnp.float32), axis=0).astype(jnp.bfloat16)
    for n in range(copies_ref.shape[0]):
        copies_ref[n] = total


def place_kernel(place_ref, half_ref, *refs):
    refs[-1][...] = half_ref[...].astype(jnp.float32)


def placed(place, half, side, whole):
    rows, width = half.shape
    given = [] if whole is None else [whole]
    return pl.pallas_call(
        place_kernel,
        out_shape=shape((2 * rows, width), jnp.float32),
        grid_spec=pltpu.PrefetchScalarGridSpec(
            num_scalar_prefetch=1,
            grid=(1,),
            in_specs=[pl.BlockSpec((rows, width), lambda i, at: (0, 0))]
            + [pl.BlockSpec(memory_space=pl.ANY)] * len(given),
            out_specs=pl.BlockSpec((rows, width), lambda i, at: ((at[1] + side) % 2, 0)),
        ),
        input_output_aliases={2: 0} if given else {},
        compiler_params=pltpu.CompilerParams(vmem_limit_bytes=8 * MIB),
        cost_estimate=pl.CostEstimate(
            flops=0, bytes_accessed=6 * rows * width, transcendentals=0
        ),
    )(place, half, *given)


def text_grad_kernel(text_ref, home_ref, arrived_ref, grad_ref):
    grad = home_ref[...] + arrived_ref[...].astype(jnp.float32)
    text = text_ref[...].astype(jnp.float32)
    scale = lax.rsqrt(jnp.sum(text * text, axis=1, keepdims=True) + EPS)
    text = text * scale
    along = jnp.sum(text * grad, axis=1, keepdims=True)
    grad_ref[...] = (grad - text * along) * scale


def body(audio_features, proj_weight, text_raw, positive):
    rows, channels = audio_features.shape
    width = text_raw.shape[1]
    chips = lax.axis_size("zh")
    blocks = chips * lax.axis_size("core")
    place = jnp.stack([lax.axis_index("zh"), lax.axis_index("core")]).astype(jnp.int32)
    bf16, f32 = jnp.bfloat16, jnp.float32
    pair_flops = 2 * rows * rows * blocks * width
    half = channels // 2
    block = shape((rows, width), f32)
    block_b = shape((rows, width), bf16)

    (sent,) = call(text_kernel, (shape((rows + TAIL, width), bf16),), text_raw)
    own = lax.all_gather(sent.astype(jnp.float16), "zh", axis=0, tiled=True).astype(bf16)
    own, audio_features = lax.optimization_barrier((own, audio_features))
    other = shifted(own, "core", 1)
    audio, audio_b, scale = call(
        audio_kernel,
        (block, block_b, shape((rows, 1), f32)),
        audio_features,
        proj_weight,
        flops=2 * rows * channels * width,
    )
    proj_grad, tiles, sent = call(
        score_kernel,
        (block_b, shape((blocks, rows, rows), bf16), shape((half + chips * rows, width), bf16)),
        place,
        audio,
        audio_b,
        scale,
        audio_features,
        positive.reshape(rows, 1),
        own,
        other,
        scratch=[pltpu.VMEM((rows, blocks * rows), f32)],
        flops=3 * pair_flops,
        limit=20,
    )
    got = shifted(sent, "core", 1)
    (weight,) = call(
        own_kernel, (shape((half, width), f32),), place, audio_features, proj_grad, light=True
    )
    (grad_features,) = call(
        features_kernel, (shape((rows, channels), bf16),), proj_grad, proj_weight, light=True
    )
    got, weight, grad_features = lax.optimization_barrier((got, weight, grad_features))
    plane = lax.axis_size(PLANE)
    column = lax.axis_size(COLUMN)
    part = half // plane
    (parts,) = call(half_kernel, (shape((plane, part, width), bf16),), weight, got, far_outs=True)
    parts, got = lax.optimization_barrier((parts, got))
    parts = exchanged(parts, PLANE)
    across, last = call(
        text_sums_kernel, (block_b, block_b), place, tiles, audio_b, got, flops=pair_flops // 2
    )
    across = shifted(across, "zh", 1)
    last = shifted(last, "zh", -1)
    parts, across, last = lax.optimization_barrier((parts, across, last))
    (parts,) = call(fold_kernel, (shape((column, part, width), bf16),), parts, far_outs=True)
    parts = exchanged(parts, COLUMN)
    to_next, home = call(
        relay_kernel,
        (block_b, block),
        place,
        tiles,
        audio_b,
        got,
        across,
        last,
        light=True,
        far=(1, 2, 3, 4, 5),
        far_outs=True,
    )
    (parts,) = call(fold_kernel, (shape((plane, part, width), bf16),), parts, far_outs=True)
    parts, to_next, home = lax.optimization_barrier((parts, to_next, home))
    weight_half = exchanged(parts, PLANE).reshape(half, width)
    arrived = shifted(to_next, "zh", 1)
    weight_half, arrived = lax.optimization_barrier((weight_half, arrived))
    there = shifted(weight_half, "core", 1)
    grad_weight = placed(place, weight_half, 0, None)
    grad_weight = placed(place, there, 1, grad_weight)
    (grad_text,) = call(text_grad_kernel, (block,), text_raw, home, arrived)
    return (grad_weight, grad_features, grad_text)


def solution(mesh):
    fine = Mesh(mesh.devices.reshape(SPLIT), FINE)
    rows = P(FINE, None)
    return jax.shard_map(
        body,
        mesh=fine,
        in_specs=(rows, P(), rows, P(FINE)),
        out_specs=(P(), rows, rows),
        check_vma=False,
    )
```

```python
import jax
import jax.numpy as jnp
from jax import lax
from jax.experimental import pallas as pl
from jax.experimental.pallas import tpu as pltpu
from jax.sharding import Mesh, PartitionSpec as P

SCALE = 100.0
EPS = 1e-06
FINE = ("zh", "core", "zl", "x", "y")
SPLIT = (4, 2, 2, 4, 8)
PLANE = ("x", "y")
COLUMN = ("zh", "zl")
TAIL = 16
MIB = 1 << 20


def shifted(block, axis, distance):
    count = lax.axis_size(axis)
    return lax.ppermute(block, axis, [(i, (i + distance) % count) for i in range(count)])


def exchanged(block, axes):
    return lax.all_to_all(block, axes, split_axis=0, concat_axis=0, tiled=True)


def dot(a, b, da, db):
    return lax.dot_general(a, b, (((da,), (db,)), ((), ())), preferred_element_type=jnp.float32)


def call(kernel, outs, *args, scratch=(), flops=0, limit=16, light=False, far=(), far_outs=False):
    whole = pl.BlockSpec(memory_space=pltpu.VMEM)
    scalars = pl.BlockSpec(memory_space=pltpu.SMEM)
    hbm = pl.BlockSpec(memory_space=pltpu.HBM)
    size = 0 if light else sum(a.size * a.dtype.itemsize for a in (*args, *outs))
    args = [
        pltpu.with_memory_space_constraint(a, pltpu.HBM) if n in far else a
        for n, a in enumerate(args)
    ]
    staged = [args[n] for n in far] + (list(outs) if far_outs else [])

    def staging(*refs):
        refs = list(refs)
        sems = refs.pop() if staged else None
        count = len(refs) - len(staged)
        refs, buffers = refs[:count], refs[count:]
        moves = []
        for n, at in enumerate(far):
            moves.append(pltpu.make_async_copy(refs[at], buffers[n], sems.at[n]))
            refs[at] = buffers[n]
        for move in moves:
            move.start()
        for move in moves:
            move.wait()
        moves = []
        if far_outs:
            for n in range(len(far), len(staged)):
                at = len(args) + n - len(far)
                moves.append(pltpu.make_async_copy(buffers[n], refs[at], sems.at[n]))
                refs[at] = buffers[n]
        kernel(*refs)
        for move in moves:
            move.start()
        for move in moves:
            move.wait()

    buffers = [pltpu.VMEM(a.shape, a.dtype) for a in staged]
    if staged:
        buffers.append(pltpu.SemaphoreType.DMA((len(staged),)))
    return pl.pallas_call(
        staging,
        out_shape=[pltpu.HBM(a.shape, a.dtype) for a in outs] if far_outs else outs,
        in_specs=[
            scalars if a.shape == (2,) else hbm if n in far else whole for n, a in enumerate(args)
        ],
        out_specs=[hbm if far_outs else whole] * len(outs),
        scratch_shapes=[*scratch, *buffers],
        compiler_params=pltpu.CompilerParams(vmem_limit_bytes=limit * MIB),
        cost_estimate=pl.CostEstimate(flops=flops, bytes_accessed=size, transcendentals=0),
    )(*args)


def shape(dims, dtype):
    return jax.ShapeDtypeStruct(dims, dtype)


def text_kernel(text_ref, sent_ref):
    rows = text_ref.shape[0]
    text = text_ref[...].astype(jnp.float32)
    scale = lax.rsqrt(jnp.sum(text * text, axis=1, keepdims=True) + EPS)
    text = (text * scale).astype(jnp.bfloat16).astype(jnp.float32)
    largest = jnp.max(jnp.max(jnp.abs(text), axis=1, keepdims=True), axis=0, keepdims=True)
    power = jnp.floor(jnp.log2(jnp.maximum(largest, 1e-30))) - 13.0
    sent_ref[:rows, :] = (text * jnp.exp2(-power)).astype(jnp.bfloat16)
    tail = (sent_ref.shape[0] - rows, sent_ref.shape[1])
    sent_ref[rows:, :] = jnp.broadcast_to(power, tail).astype(jnp.bfloat16)


def audio_kernel(features_ref, weight_ref, audio_ref, audio_b_ref, scale_ref):
    proj = dot(features_ref[...], weight_ref[...], 1, 0)
    scale = lax.rsqrt(jnp.sum(proj * proj, axis=1, keepdims=True) + EPS)
    audio = proj * scale
    audio_ref[...] = audio
    audio_b_ref[...] = audio.astype(jnp.bfloat16)
    scale_ref[...] = scale


def score_kernel(
    place_ref, audio_ref, audio_b_ref, scale_ref, features_ref, positive_ref, own_ref, other_ref,
    grad_ref, tiles_ref, sent_ref, scores_ref,
):
    core = place_ref[1]
    blocks, rows, _ = tiles_ref.shape
    chips = blocks // 2
    audio_b = audio_b_ref[...]

    def text(n):
        held = own_ref if n < chips else other_ref
        start = n % chips * (rows + TAIL)
        power = held[start + rows : start + rows + TAIL, :128].astype(jnp.float32)
        return held[start : start + rows, :], SCALE * jnp.exp2(power[:1, :1])

    for n in range(blocks):
        block, scale = text(n)
        scores_ref[:, n * rows : (n + 1) * rows] = scale * dot(audio_b, block, 1, 1)
    step = 16
    ids = lax.broadcasted_iota(jnp.int32, (step, rows), 1)
    for r in range(0, rows, step):
        scores = scores_ref[r : r + step, :]
        weights = jnp.exp(scores - jnp.max(scores, axis=1, keepdims=True))
        weights = weights * (1.0 / jnp.sum(weights, axis=1, keepdims=True))
        positive = positive_ref[r : r + step, :]
        for n in range(blocks):
            column = core if n < chips else 1 - core
            first = ((n % chips) * 2 + column) * rows
            match = jnp.where(positive - first == ids, 1.0, 0.0)
            part = weights[:, n * rows : (n + 1) * rows] - match
            tiles_ref[n, r : r + step, :] = part.astype(jnp.bfloat16)
    total = jnp.zeros(audio_ref.shape, jnp.float32)
    for n in range(blocks):
        block, scale = text(n)
        total = total + scale * dot(tiles_ref[n], block, 1, 0)
    audio = audio_ref[...]
    along = jnp.sum(audio * total, axis=1, keepdims=True)
    grad = ((total - audio * along) * scale_ref[...]).astype(jnp.bfloat16)
    grad_ref[...] = grad
    half = features_ref.shape[1] // 2
    features = features_ref[:, pl.ds(pl.multiple_of((1 - core) * half, half), half)]
    sent_ref[:half, :] = dot(features, grad, 0, 0).astype(jnp.bfloat16)
    for n in range(chips):
        part = SCALE * dot(tiles_ref[chips + n], audio_b, 0, 0)
        sent_ref[half + n * rows : half + (n + 1) * rows, :] = part.astype(jnp.bfloat16)


def own_kernel(place_ref, features_ref, grad_ref, weight_ref):
    half = features_ref.shape[1] // 2
    features = features_ref[:, pl.ds(pl.multiple_of(place_ref[1] * half, half), half)]
    weight_ref[...] = dot(features, grad_ref[...], 0, 0)


def half_kernel(weight_ref, got_ref, half_ref):
    parts, rows, width = half_ref.shape
    total = weight_ref[...] + got_ref[: parts * rows, :].astype(jnp.float32)
    half_ref[...] = total.astype(jnp.bfloat16).reshape(parts, rows, width)


def features_kernel(grad_ref, weight_ref, out_ref):
    out_ref[...] = dot(grad_ref[...], weight_ref[...], 1, 1).astype(jnp.bfloat16)


def summed(place_ref, tiles_ref, audio_b_ref, got_ref, distance):
    chips, rows = tiles_ref.shape[0] // 2, tiles_ref.shape[2]
    to = lax.rem(place_ref[0] + distance, chips)
    start = pl.multiple_of(got_ref.shape[0] - chips * rows + to * rows, rows)
    part = SCALE * dot(tiles_ref[to], audio_b_ref[...], 0, 0)
    return part + got_ref[pl.ds(start, rows), :].astype(jnp.float32)


def text_sums_kernel(place_ref, tiles_ref, audio_b_ref, got_ref, forward_ref, backward_ref):
    across = summed(place_ref, tiles_ref, audio_b_ref, got_ref, 2).astype(jnp.bfloat16)
    cut = forward_ref.shape[0]
    forward_ref[...] = across[:cut]
    backward_ref[...] = across[cut:]


def relay_kernel(
    place_ref, tiles_ref, audio_b_ref, got_ref, forward_ref, backward_ref, to_next_ref, to_last_ref
):
    refs = (place_ref, tiles_ref, audio_b_ref, got_ref)
    cut = forward_ref.shape[0]
    ahead, behind = summed(*refs, 1), summed(*refs, 3)
    to_next_ref[:cut, :] = (ahead[:cut] + forward_ref[...].astype(jnp.float32)).astype(jnp.bfloat16)
    to_next_ref[cut:, :] = ahead[cut:].astype(jnp.bfloat16)
    to_last_ref[:cut, :] = behind[:cut].astype(jnp.bfloat16)
    to_last_ref[cut:, :] = (behind[cut:] + backward_ref[...].astype(jnp.float32)).astype(jnp.bfloat16)


def home_kernel(place_ref, tiles_ref, audio_b_ref, got_ref, home_ref):
    home_ref[...] = summed(place_ref, tiles_ref, audio_b_ref, got_ref, 0)


def fold_kernel(parts_ref, copies_ref):
    total = jnp.sum(parts_ref[...].astype(jnp.float32), axis=0).astype(jnp.bfloat16)
    for n in range(copies_ref.shape[0]):
        copies_ref[n] = total


def place_kernel(place_ref, half_ref, *refs):
    refs[-1][...] = half_ref[...].astype(jnp.float32)


def placed(place, half, side, whole):
    rows, width = half.shape
    given = [] if whole is None else [whole]
    return pl.pallas_call(
        place_kernel,
        out_shape=shape((2 * rows, width), jnp.float32),
        grid_spec=pltpu.PrefetchScalarGridSpec(
            num_scalar_prefetch=1,
            grid=(1,),
            in_specs=[pl.BlockSpec((rows, width), lambda i, at: (0, 0))]
            + [pl.BlockSpec(memory_space=pl.ANY)] * len(given),
            out_specs=pl.BlockSpec((rows, width), lambda i, at: ((at[1] + side) % 2, 0)),
        ),
        input_output_aliases={2: 0} if given else {},
        compiler_params=pltpu.CompilerParams(vmem_limit_bytes=8 * MIB),
        cost_estimate=pl.CostEstimate(
            flops=0, bytes_accessed=6 * rows * width, transcendentals=0
        ),
    )(place, half, *given)


def text_grad_kernel(text_ref, home_ref, next_ref, last_ref, grad_ref):
    grad = home_ref[...] + (next_ref[...].astype(jnp.float32) + last_ref[...].astype(jnp.float32))
    text = text_ref[...].astype(jnp.float32)
    scale = lax.rsqrt(jnp.sum(text * text, axis=1, keepdims=True) + EPS)
    text = text * scale
    along = jnp.sum(text * grad, axis=1, keepdims=True)
    grad_ref[...] = (grad - text * along) * scale


def body(audio_features, proj_weight, text_raw, positive):
    rows, channels = audio_features.shape
    width = text_raw.shape[1]
    chips = lax.axis_size("zh")
    blocks = chips * lax.axis_size("core")
    place = jnp.stack([lax.axis_index("zh"), lax.axis_index("core")]).astype(jnp.int32)
    bf16, f32 = jnp.bfloat16, jnp.float32
    pair_flops = 2 * rows * rows * blocks * width
    half = channels // 2
    block = shape((rows, width), f32)
    block_b = shape((rows, width), bf16)
    cut_b = shape((rows // 2, width), bf16)

    (sent,) = call(text_kernel, (shape((rows + TAIL, width), bf16),), text_raw)
    own = lax.all_gather(sent.astype(jnp.float16), "zh", axis=0, tiled=True).astype(bf16)
    own, audio_features = lax.optimization_barrier((own, audio_features))
    other = shifted(own, "core", 1)
    audio, audio_b, scale = call(
        audio_kernel,
        (block, block_b, shape((rows, 1), f32)),
        audio_features,
        proj_weight,
        flops=2 * rows * channels * width,
    )
    proj_grad, tiles, sent = call(
        score_kernel,
        (block_b, shape((blocks, rows, rows), bf16), shape((half + chips * rows, width), bf16)),
        place,
        audio,
        audio_b,
        scale,
        audio_features,
        positive.reshape(rows, 1),
        own,
        other,
        scratch=[pltpu.VMEM((rows, blocks * rows), f32)],
        flops=3 * pair_flops,
        limit=20,
    )
    got = shifted(sent, "core", 1)
    (weight,) = call(
        own_kernel, (shape((half, width), f32),), place, audio_features, proj_grad, light=True
    )
    (grad_features,) = call(
        features_kernel, (shape((rows, channels), bf16),), proj_grad, proj_weight, light=True
    )
    got, weight, grad_features = lax.optimization_barrier((got, weight, grad_features))
    plane = lax.axis_size(PLANE)
    column = lax.axis_size(COLUMN)
    part = half // plane
    (parts,) = call(half_kernel, (shape((plane, part, width), bf16),), weight, got, far_outs=True)
    parts, got = lax.optimization_barrier((parts, got))
    parts = exchanged(parts, PLANE)
    forward, backward = call(
        text_sums_kernel, (cut_b, cut_b), place, tiles, audio_b, got, flops=pair_flops // 4
    )
    forward = shifted(forward, "zh", 1)
    backward = shifted(backward, "zh", -1)
    parts, forward, backward = lax.optimization_barrier((parts, forward, backward))
    (parts,) = call(fold_kernel, (shape((column, part, width), bf16),), parts, far_outs=True)
    parts = exchanged(parts, COLUMN)
    to_next, to_last = call(
        relay_kernel,
        (block_b, block_b),
        place,
        tiles,
        audio_b,
        got,
        forward,
        backward,
        light=True,
        far=(1, 2, 3, 4, 5),
        far_outs=True,
    )
    (parts,) = call(fold_kernel, (shape((plane, part, width), bf16),), parts, far_outs=True)
    parts, to_next, to_last, tiles = lax.optimization_barrier((parts, to_next, to_last, tiles))
    weight_half = exchanged(parts, PLANE).reshape(half, width)
    arrived = [shifted(to_next, "zh", 1), shifted(to_last, "zh", -1)]
    (home,) = call(
        home_kernel,
        (block,),
        place,
        tiles,
        audio_b,
        got,
        light=True,
        far=(1, 2, 3),
        far_outs=True,
    )
    weight_half, arrived, home = lax.optimization_barrier((weight_half, arrived, home))
    there = shifted(weight_half, "core", 1)
    grad_weight = placed(place, weight_half, 0, None)
    grad_weight = placed(place, there, 1, grad_weight)
    (grad_text,) = call(text_grad_kernel, (block,), text_raw, home, *arrived)
    return (grad_weight, grad_features, grad_text)


def solution(mesh):
    fine = Mesh(mesh.devices.reshape(SPLIT), FINE)
    rows = P(FINE, None)
    return jax.shard_map(
        body,
        mesh=fine,
        in_specs=(rows, P(), rows, P(FINE)),
        out_specs=(P(), rows, rows),
        check_vma=False,
    )
```

```python
import functools

import jax
import jax.numpy as jnp
from jax import lax
from jax.experimental import pallas as pl
from jax.experimental.pallas import tpu as pltpu
from jax.sharding import Mesh, PartitionSpec as P

SCALE = 100.0
EPS = 1e-06
FINE = ("zh", "core", "zl", "x", "y")
SPLIT = (4, 2, 2, 4, 8)
PLANE = ("x", "y")
COLUMN = ("zh", "zl")
TAIL = 16
EARLY = 64
MIB = 1 << 20


def shifted(block, axis, distance):
    count = lax.axis_size(axis)
    return lax.ppermute(block, axis, [(i, (i + distance) % count) for i in range(count)])


def exchanged(block, axes):
    return lax.all_to_all(block, axes, split_axis=0, concat_axis=0, tiled=True)


def dot(a, b, da, db):
    return lax.dot_general(a, b, (((da,), (db,)), ((), ())), preferred_element_type=jnp.float32)


def call(kernel, outs, *args, scratch=(), flops=0, limit=16, light=False, far=(), far_outs=False):
    whole = pl.BlockSpec(memory_space=pltpu.VMEM)
    scalars = pl.BlockSpec(memory_space=pltpu.SMEM)
    hbm = pl.BlockSpec(memory_space=pltpu.HBM)
    size = 0 if light else sum(a.size * a.dtype.itemsize for a in (*args, *outs))
    args = [
        pltpu.with_memory_space_constraint(a, pltpu.HBM) if n in far else a
        for n, a in enumerate(args)
    ]
    staged = [args[n] for n in far] + (list(outs) if far_outs else [])

    def staging(*refs):
        refs = list(refs)
        sems = refs.pop() if staged else None
        count = len(refs) - len(staged)
        refs, buffers = refs[:count], refs[count:]
        moves = []
        for n, at in enumerate(far):
            moves.append(pltpu.make_async_copy(refs[at], buffers[n], sems.at[n]))
            refs[at] = buffers[n]
        for move in moves:
            move.start()
        for move in moves:
            move.wait()
        moves = []
        if far_outs:
            for n in range(len(far), len(staged)):
                at = len(args) + n - len(far)
                moves.append(pltpu.make_async_copy(buffers[n], refs[at], sems.at[n]))
                refs[at] = buffers[n]
        kernel(*refs)
        for move in moves:
            move.start()
        for move in moves:
            move.wait()

    buffers = [pltpu.VMEM(a.shape, a.dtype) for a in staged]
    if staged:
        buffers.append(pltpu.SemaphoreType.DMA((len(staged),)))
    return pl.pallas_call(
        staging,
        out_shape=[pltpu.HBM(a.shape, a.dtype) for a in outs] if far_outs else outs,
        in_specs=[
            scalars if a.shape == (2,) else hbm if n in far else whole for n, a in enumerate(args)
        ],
        out_specs=[hbm if far_outs else whole] * len(outs),
        scratch_shapes=[*scratch, *buffers],
        compiler_params=pltpu.CompilerParams(vmem_limit_bytes=limit * MIB),
        cost_estimate=pl.CostEstimate(flops=flops, bytes_accessed=size, transcendentals=0),
    )(*args)


def shape(dims, dtype):
    return jax.ShapeDtypeStruct(dims, dtype)


def text_kernel(text_ref, sent_ref):
    rows = text_ref.shape[0]
    text = text_ref[...].astype(jnp.float32)
    scale = lax.rsqrt(jnp.sum(text * text, axis=1, keepdims=True) + EPS)
    text = (text * scale).astype(jnp.bfloat16).astype(jnp.float32)
    largest = jnp.max(jnp.max(jnp.abs(text), axis=1, keepdims=True), axis=0, keepdims=True)
    power = jnp.floor(jnp.log2(jnp.maximum(largest, 1e-30))) - 13.0
    sent_ref[:rows, :] = (text * jnp.exp2(-power)).astype(jnp.bfloat16)
    tail = (sent_ref.shape[0] - rows, sent_ref.shape[1])
    sent_ref[rows:, :] = jnp.broadcast_to(power, tail).astype(jnp.bfloat16)


def text_block(held_ref, n, rows):
    start = n * (rows + TAIL)
    power = held_ref[start + rows : start + rows + TAIL, :128].astype(jnp.float32)
    return held_ref[start : start + rows, :], SCALE * jnp.exp2(power[:1, :1])


def audio_kernel(
    features_ref, weight_ref, own_ref, audio_ref, audio_b_ref, scale_ref, scores_ref
):
    rows = audio_ref.shape[0]
    proj = dot(features_ref[...], weight_ref[...], 1, 0)
    scale = lax.rsqrt(jnp.sum(proj * proj, axis=1, keepdims=True) + EPS)
    audio = proj * scale
    audio_b = audio.astype(jnp.bfloat16)
    audio_ref[...] = audio
    audio_b_ref[...] = audio_b
    scale_ref[...] = scale
    for n in range(scores_ref.shape[1] // rows):
        block, factor = text_block(own_ref, n, rows)
        scores_ref[:, n * rows : (n + 1) * rows] = factor * dot(audio_b, block, 1, 1)


def score_kernel(
    place_ref, audio_ref, audio_b_ref, scale_ref, features_ref, positive_ref, own_ref, other_ref,
    own_scores_ref, grad_ref, tiles_ref, sent_ref, scores_ref,
):
    core = place_ref[1]
    blocks, rows, _ = tiles_ref.shape
    chips = blocks // 2
    audio_b = audio_b_ref[...]
    for n in range(chips):
        block, factor = text_block(other_ref, n, rows)
        scores_ref[:, n * rows : (n + 1) * rows] = factor * dot(audio_b, block, 1, 1)
    step = 16
    ids = lax.broadcasted_iota(jnp.int32, (step, rows), 1)
    for r in range(0, rows, step):
        both = [own_scores_ref[r : r + step, :], scores_ref[r : r + step, :]]
        peak = jnp.maximum(*(jnp.max(scores, axis=1, keepdims=True) for scores in both))
        both = [jnp.exp(scores - peak) for scores in both]
        share = 1.0 / sum(jnp.sum(weights, axis=1, keepdims=True) for weights in both)
        positive = positive_ref[r : r + step, :]
        for n in range(blocks):
            column = core if n < chips else 1 - core
            first = ((n % chips) * 2 + column) * rows
            match = jnp.where(positive - first == ids, 1.0, 0.0)
            lanes = slice(n % chips * rows, (n % chips + 1) * rows)
            part = both[n // chips][:, lanes] * share - match
            tiles_ref[n, r : r + step, :] = part.astype(jnp.bfloat16)
    total = jnp.zeros(audio_ref.shape, jnp.float32)
    for n in range(blocks):
        block, factor = text_block(own_ref if n < chips else other_ref, n % chips, rows)
        total = total + factor * dot(tiles_ref[n], block, 1, 0)
    audio = audio_ref[...]
    along = jnp.sum(audio * total, axis=1, keepdims=True)
    grad = ((total - audio * along) * scale_ref[...]).astype(jnp.bfloat16)
    grad_ref[...] = grad
    half = features_ref.shape[1] // 2
    features = features_ref[:, pl.ds(pl.multiple_of((1 - core) * half, half), half)]
    sent_ref[:half, :] = dot(features, grad, 0, 0).astype(jnp.bfloat16)
    for n in range(chips):
        part = SCALE * dot(tiles_ref[chips + n], audio_b, 0, 0)
        sent_ref[half + n * rows : half + (n + 1) * rows, :] = part.astype(jnp.bfloat16)


def own_kernel(place_ref, features_ref, grad_ref, weight_ref):
    half = features_ref.shape[1] // 2
    features = features_ref[:, pl.ds(pl.multiple_of(place_ref[1] * half, half), half)]
    weight_ref[...] = dot(features, grad_ref[...], 0, 0)


def half_kernel(weight_ref, got_ref, half_ref):
    parts, rows, width = half_ref.shape
    total = weight_ref[...] + got_ref[: parts * rows, :].astype(jnp.float32)
    half_ref[...] = total.astype(jnp.bfloat16).reshape(parts, rows, width)


def features_kernel(grad_ref, weight_ref, out_ref):
    out_ref[...] = dot(grad_ref[...], weight_ref[...], 1, 1).astype(jnp.bfloat16)


def summed(place_ref, tiles_ref, audio_b_ref, got_ref, distance):
    chips, rows = tiles_ref.shape[0] // 2, tiles_ref.shape[2]
    to = lax.rem(place_ref[0] + distance, chips)
    start = pl.multiple_of(got_ref.shape[0] - chips * rows + to * rows, rows)
    part = SCALE * dot(tiles_ref[to], audio_b_ref[...], 0, 0)
    return part + got_ref[pl.ds(start, rows), :].astype(jnp.float32)


def text_sums_kernel(place_ref, tiles_ref, audio_b_ref, got_ref, forward_ref, backward_ref):
    refs = (place_ref, tiles_ref, audio_b_ref, got_ref)
    rows = tiles_ref.shape[2]
    cut = rows // 2
    across = summed(*refs, 2).astype(jnp.bfloat16)
    forward_ref[:cut, :] = across[:cut]
    backward_ref[:cut, :] = across[cut:]
    forward_ref[cut:, :] = summed(*refs, 1)[rows - EARLY :].astype(jnp.bfloat16)
    backward_ref[cut:, :] = summed(*refs, 3)[:EARLY].astype(jnp.bfloat16)


def relay_kernel(
    place_ref, tiles_ref, audio_b_ref, got_ref, forward_ref, backward_ref, to_next_ref, to_last_ref
):
    refs = (place_ref, tiles_ref, audio_b_ref, got_ref)
    rows = tiles_ref.shape[2]
    cut = rows // 2
    forward = forward_ref[:cut, :].astype(jnp.float32)
    backward = backward_ref[:cut, :].astype(jnp.float32)
    ahead, behind = summed(*refs, 1), summed(*refs, 3)
    to_next_ref[:cut, :] = (ahead[:cut] + forward).astype(jnp.bfloat16)
    to_next_ref[cut:, :] = ahead[cut : rows - EARLY].astype(jnp.bfloat16)
    to_last_ref[: cut - EARLY, :] = behind[EARLY:cut].astype(jnp.bfloat16)
    to_last_ref[cut - EARLY :, :] = (behind[cut:] + backward).astype(jnp.bfloat16)


def home_kernel(
    place_ref, tiles_ref, audio_b_ref, got_ref, forward_ref, backward_ref, home_ref
):
    home = summed(place_ref, tiles_ref, audio_b_ref, got_ref, 0)
    rows = home.shape[0]
    forward = forward_ref[rows // 2 :, :].astype(jnp.float32)
    backward = backward_ref[rows // 2 :, :].astype(jnp.float32)
    home_ref[:EARLY, :] = home[:EARLY] + backward
    home_ref[EARLY : rows - EARLY, :] = home[EARLY : rows - EARLY]
    home_ref[rows - EARLY :, :] = home[rows - EARLY :] + forward


def fold_kernel(parts_ref, copies_ref):
    total = jnp.sum(parts_ref[...].astype(jnp.float32), axis=0).astype(jnp.bfloat16)
    for n in range(copies_ref.shape[0]):
        copies_ref[n] = total


def place_kernel(side, place_ref, half_ref, *refs):
    whole_ref, buffer, sems = refs[-3:]
    pieces = sems.shape[0]
    rows = half_ref.shape[0]
    step = rows // pieces
    first = lax.rem(place_ref[1] + side, 2) * rows
    moves = []
    for n in range(pieces):
        part = pl.ds(n * step, step)
        buffer[part, :] = half_ref[part, :].astype(jnp.float32)
        to = pl.ds(pl.multiple_of(first + n * step, step), step)
        moves.append(pltpu.make_async_copy(buffer.at[part, :], whole_ref.at[to, :], sems.at[n]))
        moves[-1].start()
    for move in moves:
        move.wait()


def placed(place, half, side, whole):
    rows, width = half.shape
    given = [] if whole is None else [whole]
    return pl.pallas_call(
        functools.partial(place_kernel, side),
        out_shape=shape((2 * rows, width), jnp.float32),
        in_specs=[
            pl.BlockSpec(memory_space=pltpu.SMEM),
            pl.BlockSpec(memory_space=pltpu.VMEM),
            *[pl.BlockSpec(memory_space=pl.ANY)] * len(given),
        ],
        out_specs=pl.BlockSpec(memory_space=pl.ANY),
        scratch_shapes=[pltpu.VMEM((rows, width), jnp.float32), pltpu.SemaphoreType.DMA((4,))],
        input_output_aliases={2: 0} if given else {},
        compiler_params=pltpu.CompilerParams(vmem_limit_bytes=8 * MIB),
        cost_estimate=pl.CostEstimate(
            flops=0, bytes_accessed=6 * rows * width, transcendentals=0
        ),
    )(place, half, *given)


def text_grad_kernel(text_ref, home_ref, next_ref, last_ref, grad_ref):
    rows, late = home_ref.shape[0], next_ref.shape[0]
    home = home_ref[...]
    ahead, behind = next_ref[...].astype(jnp.float32), last_ref[...].astype(jnp.float32)
    middle = home[rows - late : late] + ahead[rows - late :] + behind[: 2 * late - rows]
    first, final = home[: rows - late] + ahead[: rows - late], home[late:] + behind[2 * late - rows :]
    grad = jnp.concatenate([first, middle, final])
    text = text_ref[...].astype(jnp.float32)
    scale = lax.rsqrt(jnp.sum(text * text, axis=1, keepdims=True) + EPS)
    text = text * scale
    along = jnp.sum(text * grad, axis=1, keepdims=True)
    grad_ref[...] = (grad - text * along) * scale


def body(audio_features, proj_weight, text_raw, positive):
    rows, channels = audio_features.shape
    width = text_raw.shape[1]
    chips = lax.axis_size("zh")
    blocks = chips * lax.axis_size("core")
    place = jnp.stack([lax.axis_index("zh"), lax.axis_index("core")]).astype(jnp.int32)
    bf16, f32 = jnp.bfloat16, jnp.float32
    pair_flops = 2 * rows * rows * blocks * width
    half = channels // 2
    block = shape((rows, width), f32)
    block_b = shape((rows, width), bf16)
    early_b = shape((rows // 2 + EARLY, width), bf16)
    late_b = shape((rows - EARLY, width), bf16)

    (sent,) = call(text_kernel, (shape((rows + TAIL, width), bf16),), text_raw)
    own = lax.all_gather(sent.astype(jnp.float16), "zh", axis=0, tiled=True).astype(bf16)
    own, audio_features = lax.optimization_barrier((own, audio_features))
    other = shifted(own, "core", 1)
    audio, audio_b, scale, own_scores = call(
        audio_kernel,
        (block, block_b, shape((rows, 1), f32), shape((rows, chips * rows), f32)),
        audio_features,
        proj_weight,
        own,
        flops=2 * rows * channels * width,
    )
    proj_grad, tiles, sent = call(
        score_kernel,
        (block_b, shape((blocks, rows, rows), bf16), shape((half + chips * rows, width), bf16)),
        place,
        audio,
        audio_b,
        scale,
        audio_features,
        positive.reshape(rows, 1),
        own,
        other,
        own_scores,
        scratch=[pltpu.VMEM((rows, chips * rows), f32)],
        flops=3 * pair_flops,
        limit=20,
    )
    got = shifted(sent, "core", 1)
    (weight,) = call(
        own_kernel, (shape((half, width), f32),), place, audio_features, proj_grad, light=True
    )
    (grad_features,) = call(
        features_kernel, (shape((rows, channels), bf16),), proj_grad, proj_weight, light=True
    )
    got, weight, grad_features = lax.optimization_barrier((got, weight, grad_features))
    plane = lax.axis_size(PLANE)
    column = lax.axis_size(COLUMN)
    part = half // plane
    (parts,) = call(half_kernel, (shape((plane, part, width), bf16),), weight, got, far_outs=True)
    parts, got = lax.optimization_barrier((parts, got))
    parts = exchanged(parts, PLANE)
    forward, backward = call(
        text_sums_kernel, (early_b, early_b), place, tiles, audio_b, got, flops=pair_flops // 4
    )
    forward = shifted(forward, "zh", 1)
    backward = shifted(backward, "zh", -1)
    parts, forward, backward = lax.optimization_barrier((parts, forward, backward))
    (parts,) = call(fold_kernel, (shape((column, part, width), bf16),), parts, far_outs=True)
    parts = exchanged(parts, COLUMN)
    to_next, to_last = call(
        relay_kernel,
        (late_b, late_b),
        place,
        tiles,
        audio_b,
        got,
        forward,
        backward,
        light=True,
        far=(1, 2, 3, 4, 5),
        far_outs=True,
    )
    (parts,) = call(fold_kernel, (shape((plane, part, width), bf16),), parts, far_outs=True)
    parts, to_next, to_last, tiles = lax.optimization_barrier((parts, to_next, to_last, tiles))
    weight_half = exchanged(parts, PLANE).reshape(half, width)
    arrived = [shifted(to_next, "zh", 1), shifted(to_last, "zh", -1)]
    (home,) = call(
        home_kernel,
        (block,),
        place,
        tiles,
        audio_b,
        got,
        forward,
        backward,
        light=True,
        far=(1, 2, 3, 4, 5),
        far_outs=True,
    )
    weight_half, arrived, home = lax.optimization_barrier((weight_half, arrived, home))
    there = shifted(weight_half, "core", 1)
    grad_weight = placed(place, weight_half, 0, None)
    grad_weight = placed(place, there, 1, grad_weight)
    (grad_text,) = call(text_grad_kernel, (block,), text_raw, home, *arrived)
    return (grad_weight, grad_features, grad_text)


def solution(mesh):
    fine = Mesh(mesh.devices.reshape(SPLIT), FINE)
    rows = P(FINE, None)
    return jax.shard_map(
        body,
        mesh=fine,
        in_specs=(rows, P(), rows, P(FINE)),
        out_specs=(P(), rows, rows),
        check_vma=False,
    )
```

```python
import functools

import jax
import jax.numpy as jnp
from jax import lax
from jax.experimental import pallas as pl
from jax.experimental.pallas import tpu as pltpu
from jax.sharding import Mesh, PartitionSpec as P

SCALE = 100.0
EPS = 1e-06
FINE = ("zh", "core", "zl", "x", "y")
SPLIT = (4, 2, 2, 4, 8)
PLANE = ("x", "y")
COLUMN = ("zh", "zl")
TAIL = 16
EARLY = 64
MIB = 1 << 20


def shifted(block, axis, distance):
    count = lax.axis_size(axis)
    return lax.ppermute(block, axis, [(i, (i + distance) % count) for i in range(count)])


def exchanged(block, axes):
    return lax.all_to_all(block, axes, split_axis=0, concat_axis=0, tiled=True)


def dot(a, b, da, db):
    return lax.dot_general(a, b, (((da,), (db,)), ((), ())), preferred_element_type=jnp.float32)


def call(kernel, outs, *args, scratch=(), flops=0, limit=16, light=False, far=(), far_outs=False):
    whole = pl.BlockSpec(memory_space=pltpu.VMEM)
    scalars = pl.BlockSpec(memory_space=pltpu.SMEM)
    hbm = pl.BlockSpec(memory_space=pltpu.HBM)
    size = 0 if light else sum(a.size * a.dtype.itemsize for a in (*args, *outs))
    args = [
        pltpu.with_memory_space_constraint(a, pltpu.HBM) if n in far else a
        for n, a in enumerate(args)
    ]
    staged = [args[n] for n in far] + (list(outs) if far_outs else [])

    def staging(*refs):
        refs = list(refs)
        sems = refs.pop() if staged else None
        count = len(refs) - len(staged)
        refs, buffers = refs[:count], refs[count:]
        moves = []
        for n, at in enumerate(far):
            moves.append(pltpu.make_async_copy(refs[at], buffers[n], sems.at[n]))
            refs[at] = buffers[n]
        for move in moves:
            move.start()
        for move in moves:
            move.wait()
        moves = []
        if far_outs:
            for n in range(len(far), len(staged)):
                at = len(args) + n - len(far)
                moves.append(pltpu.make_async_copy(buffers[n], refs[at], sems.at[n]))
                refs[at] = buffers[n]
        kernel(*refs)
        for move in moves:
            move.start()
        for move in moves:
            move.wait()

    buffers = [pltpu.VMEM(a.shape, a.dtype) for a in staged]
    if staged:
        buffers.append(pltpu.SemaphoreType.DMA((len(staged),)))
    return pl.pallas_call(
        staging,
        out_shape=[pltpu.HBM(a.shape, a.dtype) for a in outs] if far_outs else outs,
        in_specs=[
            scalars if a.shape == (2,) else hbm if n in far else whole for n, a in enumerate(args)
        ],
        out_specs=[hbm if far_outs else whole] * len(outs),
        scratch_shapes=[*scratch, *buffers],
        compiler_params=pltpu.CompilerParams(vmem_limit_bytes=limit * MIB),
        cost_estimate=pl.CostEstimate(flops=flops, bytes_accessed=size, transcendentals=0),
    )(*args)


def shape(dims, dtype):
    return jax.ShapeDtypeStruct(dims, dtype)


def text_kernel(text_ref, sent_ref):
    rows = text_ref.shape[0]
    text = text_ref[...].astype(jnp.float32)
    scale = lax.rsqrt(jnp.sum(text * text, axis=1, keepdims=True) + EPS)
    text = (text * scale).astype(jnp.bfloat16).astype(jnp.float32)
    largest = jnp.max(jnp.max(jnp.abs(text), axis=1, keepdims=True), axis=0, keepdims=True)
    power = jnp.floor(jnp.log2(jnp.maximum(largest, 1e-30))) - 13.0
    sent_ref[:rows, :] = (text * jnp.exp2(-power)).astype(jnp.bfloat16)
    tail = (sent_ref.shape[0] - rows, sent_ref.shape[1])
    sent_ref[rows:, :] = jnp.broadcast_to(power, tail).astype(jnp.bfloat16)


def text_block(held_ref, n, rows):
    start = n * (rows + TAIL)
    power = held_ref[start + rows : start + rows + TAIL, :128].astype(jnp.float32)
    return held_ref[start : start + rows, :], SCALE * jnp.exp2(power[:1, :1])


def audio_kernel(
    features_ref, weight_ref, own_ref, audio_ref, audio_b_ref, scale_ref, scores_ref
):
    rows = audio_ref.shape[0]
    proj = dot(features_ref[...], weight_ref[...], 1, 0)
    scale = lax.rsqrt(jnp.sum(proj * proj, axis=1, keepdims=True) + EPS)
    audio = proj * scale
    audio_b = audio.astype(jnp.bfloat16)
    audio_ref[...] = audio
    audio_b_ref[...] = audio_b
    scale_ref[...] = scale
    for n in range(scores_ref.shape[1] // rows):
        block, factor = text_block(own_ref, n, rows)
        scores_ref[:, n * rows : (n + 1) * rows] = factor * dot(audio_b, block, 1, 1)


def score_kernel(
    place_ref, audio_ref, audio_b_ref, scale_ref, features_ref, positive_ref, own_ref, other_ref,
    own_scores_ref, grad_ref, tiles_ref, sent_ref, scores_ref,
):
    core = place_ref[1]
    blocks, rows, _ = tiles_ref.shape
    chips = blocks // 2
    audio_b = audio_b_ref[...]
    for n in range(chips):
        block, factor = text_block(other_ref, n, rows)
        scores_ref[:, n * rows : (n + 1) * rows] = factor * dot(audio_b, block, 1, 1)
    step = 16
    ids = lax.broadcasted_iota(jnp.int32, (step, rows), 1)
    for r in range(0, rows, step):
        both = [own_scores_ref[r : r + step, :], scores_ref[r : r + step, :]]
        peak = jnp.maximum(*(jnp.max(scores, axis=1, keepdims=True) for scores in both))
        both = [jnp.exp(scores - peak) for scores in both]
        share = 1.0 / sum(jnp.sum(weights, axis=1, keepdims=True) for weights in both)
        positive = positive_ref[r : r + step, :]
        for n in range(blocks):
            column = core if n < chips else 1 - core
            first = ((n % chips) * 2 + column) * rows
            match = jnp.where(positive - first == ids, 1.0, 0.0)
            lanes = slice(n % chips * rows, (n % chips + 1) * rows)
            part = both[n // chips][:, lanes] * share - match
            tiles_ref[n, r : r + step, :] = part.astype(jnp.bfloat16)
    total = jnp.zeros(audio_ref.shape, jnp.float32)
    for n in range(blocks):
        block, factor = text_block(own_ref if n < chips else other_ref, n % chips, rows)
        total = total + factor * dot(tiles_ref[n], block, 1, 0)
    audio = audio_ref[...]
    along = jnp.sum(audio * total, axis=1, keepdims=True)
    grad = ((total - audio * along) * scale_ref[...]).astype(jnp.bfloat16)
    grad_ref[...] = grad
    half = features_ref.shape[1] // 2
    features = features_ref[:, pl.ds(pl.multiple_of((1 - core) * half, half), half)]
    sent_ref[:half, :] = dot(features, grad, 0, 0).astype(jnp.bfloat16)
    for n in range(chips):
        part = SCALE * dot(tiles_ref[chips + n], audio_b, 0, 0)
        sent_ref[half + n * rows : half + (n + 1) * rows, :] = part.astype(jnp.bfloat16)


def own_kernel(place_ref, features_ref, grad_ref, weight_ref):
    half = features_ref.shape[1] // 2
    features = features_ref[:, pl.ds(pl.multiple_of(place_ref[1] * half, half), half)]
    weight_ref[...] = dot(features, grad_ref[...], 0, 0)


def half_kernel(weight_ref, got_ref, half_ref):
    parts, rows, width = half_ref.shape
    total = weight_ref[...] + got_ref[: parts * rows, :].astype(jnp.float32)
    half_ref[...] = total.astype(jnp.bfloat16).reshape(parts, rows, width)


def features_kernel(grad_ref, weight_ref, out_ref):
    out_ref[...] = dot(grad_ref[...], weight_ref[...], 1, 1).astype(jnp.bfloat16)


def summed(place_ref, tiles_ref, audio_b_ref, got_ref, distance):
    chips, rows = tiles_ref.shape[0] // 2, tiles_ref.shape[2]
    to = lax.rem(place_ref[0] + distance, chips)
    start = pl.multiple_of(got_ref.shape[0] - chips * rows + to * rows, rows)
    part = SCALE * dot(tiles_ref[to], audio_b_ref[...], 0, 0)
    return part + got_ref[pl.ds(start, rows), :].astype(jnp.float32)


def early_kernel(place_ref, tiles_ref, audio_b_ref, got_ref, forward_ref, backward_ref):
    refs = (place_ref, tiles_ref, audio_b_ref, got_ref)
    rows = tiles_ref.shape[2]
    cut = rows // 2
    across = summed(*refs, 2).astype(jnp.bfloat16)
    forward_ref[:cut, :] = across[:cut]
    backward_ref[:cut, :] = across[cut:]
    forward_ref[cut:, :] = summed(*refs, 1)[rows - EARLY :].astype(jnp.bfloat16)
    backward_ref[cut:, :] = summed(*refs, 3)[:EARLY].astype(jnp.bfloat16)


def late_kernel(place_ref, tiles_ref, audio_b_ref, got_ref, ahead_ref, behind_ref, home_ref):
    refs = (place_ref, tiles_ref, audio_b_ref, got_ref)
    rows = tiles_ref.shape[2]
    ahead_ref[...] = summed(*refs, 1)[: rows - EARLY]
    behind_ref[...] = summed(*refs, 3)[EARLY:]
    home_ref[...] = summed(*refs, 0)


def relay_kernel(ahead_ref, behind_ref, forward_ref, backward_ref, to_next_ref, to_last_ref):
    late = ahead_ref.shape[0]
    cut = (late + EARLY) // 2
    forward = forward_ref[:cut, :].astype(jnp.float32)
    backward = backward_ref[:cut, :].astype(jnp.float32)
    to_next_ref[:cut, :] = (ahead_ref[:cut, :] + forward).astype(jnp.bfloat16)
    to_next_ref[cut:, :] = ahead_ref[cut:, :].astype(jnp.bfloat16)
    to_last_ref[: late - cut, :] = behind_ref[: late - cut, :].astype(jnp.bfloat16)
    to_last_ref[late - cut :, :] = (behind_ref[late - cut :, :] + backward).astype(jnp.bfloat16)


def fold_kernel(parts_ref, copies_ref):
    total = jnp.sum(parts_ref[...].astype(jnp.float32), axis=0).astype(jnp.bfloat16)
    for n in range(copies_ref.shape[0]):
        copies_ref[n] = total


def place_kernel(side, place_ref, half_ref, *refs):
    whole_ref, buffer, sems = refs[-3:]
    pieces = sems.shape[0]
    rows = half_ref.shape[0]
    step = rows // pieces
    first = lax.rem(place_ref[1] + side, 2) * rows
    moves = []
    for n in range(pieces):
        part = pl.ds(n * step, step)
        buffer[part, :] = half_ref[part, :].astype(jnp.float32)
        to = pl.ds(pl.multiple_of(first + n * step, step), step)
        moves.append(pltpu.make_async_copy(buffer.at[part, :], whole_ref.at[to, :], sems.at[n]))
        moves[-1].start()
    for move in moves:
        move.wait()


def placed(place, half, side, whole):
    rows, width = half.shape
    given = [] if whole is None else [whole]
    return pl.pallas_call(
        functools.partial(place_kernel, side),
        out_shape=shape((2 * rows, width), jnp.float32),
        in_specs=[
            pl.BlockSpec(memory_space=pltpu.SMEM),
            pl.BlockSpec(memory_space=pltpu.VMEM),
            *[pl.BlockSpec(memory_space=pl.ANY)] * len(given),
        ],
        out_specs=pl.BlockSpec(memory_space=pl.ANY),
        scratch_shapes=[pltpu.VMEM((rows, width), jnp.float32), pltpu.SemaphoreType.DMA((4,))],
        input_output_aliases={2: 0} if given else {},
        compiler_params=pltpu.CompilerParams(vmem_limit_bytes=8 * MIB),
        cost_estimate=pl.CostEstimate(
            flops=0, bytes_accessed=6 * rows * width, transcendentals=0
        ),
    )(place, half, *given)


def text_grad_kernel(
    text_ref, home_ref, forward_ref, backward_ref, next_ref, last_ref, grad_ref
):
    rows, late = home_ref.shape[0], next_ref.shape[0]
    home = home_ref[...]
    forward = forward_ref[rows // 2 :, :].astype(jnp.float32)
    backward = backward_ref[rows // 2 :, :].astype(jnp.float32)
    ahead, behind = next_ref[...].astype(jnp.float32), last_ref[...].astype(jnp.float32)
    first = home[:EARLY] + ahead[:EARLY] + backward
    middle = home[EARLY:late] + ahead[EARLY:] + behind[: late - EARLY]
    final = home[late:] + forward + behind[late - EARLY :]
    grad = jnp.concatenate([first, middle, final])
    text = text_ref[...].astype(jnp.float32)
    scale = lax.rsqrt(jnp.sum(text * text, axis=1, keepdims=True) + EPS)
    text = text * scale
    along = jnp.sum(text * grad, axis=1, keepdims=True)
    grad_ref[...] = (grad - text * along) * scale


def body(audio_features, proj_weight, text_raw, positive):
    rows, channels = audio_features.shape
    width = text_raw.shape[1]
    chips = lax.axis_size("zh")
    blocks = chips * lax.axis_size("core")
    place = jnp.stack([lax.axis_index("zh"), lax.axis_index("core")]).astype(jnp.int32)
    bf16, f32 = jnp.bfloat16, jnp.float32
    pair_flops = 2 * rows * rows * blocks * width
    half = channels // 2
    block = shape((rows, width), f32)
    block_b = shape((rows, width), bf16)
    early_b = shape((rows // 2 + EARLY, width), bf16)
    late, late_b = (shape((rows - EARLY, width), dtype) for dtype in (f32, bf16))

    (sent,) = call(text_kernel, (shape((rows + TAIL, width), bf16),), text_raw)
    own = lax.all_gather(sent.astype(jnp.float16), "zh", axis=0, tiled=True).astype(bf16)
    own, audio_features = lax.optimization_barrier((own, audio_features))
    other = shifted(own, "core", 1)
    audio, audio_b, scale, own_scores = call(
        audio_kernel,
        (block, block_b, shape((rows, 1), f32), shape((rows, chips * rows), f32)),
        audio_features,
        proj_weight,
        own,
        flops=2 * rows * channels * width,
    )
    proj_grad, tiles, sent = call(
        score_kernel,
        (block_b, shape((blocks, rows, rows), bf16), shape((half + chips * rows, width), bf16)),
        place,
        audio,
        audio_b,
        scale,
        audio_features,
        positive.reshape(rows, 1),
        own,
        other,
        own_scores,
        scratch=[pltpu.VMEM((rows, chips * rows), f32)],
        flops=3 * pair_flops,
        limit=20,
    )
    got = shifted(sent, "core", 1)
    (weight,) = call(
        own_kernel, (shape((half, width), f32),), place, audio_features, proj_grad, light=True
    )
    (grad_features,) = call(
        features_kernel, (shape((rows, channels), bf16),), proj_grad, proj_weight, light=True
    )
    got, weight, grad_features = lax.optimization_barrier((got, weight, grad_features))
    plane = lax.axis_size(PLANE)
    column = lax.axis_size(COLUMN)
    part = half // plane
    (parts,) = call(half_kernel, (shape((plane, part, width), bf16),), weight, got, far_outs=True)
    parts, got = lax.optimization_barrier((parts, got))
    parts = exchanged(parts, PLANE)
    forward, backward = call(
        early_kernel, (early_b, early_b), place, tiles, audio_b, got, flops=pair_flops // 4
    )
    forward = shifted(forward, "zh", 1)
    backward = shifted(backward, "zh", -1)
    ahead, behind, home = call(
        late_kernel,
        (late, late, block),
        place,
        tiles,
        audio_b,
        got,
        flops=pair_flops,
        far_outs=True,
    )
    parts, forward, backward, ahead, behind, home = lax.optimization_barrier(
        (parts, forward, backward, ahead, behind, home)
    )
    (parts,) = call(fold_kernel, (shape((column, part, width), bf16),), parts, far_outs=True)
    parts = exchanged(parts, COLUMN)
    to_next, to_last = call(
        relay_kernel,
        (late_b, late_b),
        ahead,
        behind,
        forward,
        backward,
        light=True,
        far=(0, 1, 2, 3),
        far_outs=True,
    )
    (parts,) = call(fold_kernel, (shape((plane, part, width), bf16),), parts, far_outs=True)
    parts, to_next, to_last = lax.optimization_barrier((parts, to_next, to_last))
    weight_half = exchanged(parts, PLANE).reshape(half, width)
    arrived = [shifted(to_next, "zh", 1), shifted(to_last, "zh", -1)]
    weight_half, arrived = lax.optimization_barrier((weight_half, arrived))
    there = shifted(weight_half, "core", 1)
    grad_weight = placed(place, weight_half, 0, None)
    grad_weight = placed(place, there, 1, grad_weight)
    (grad_text,) = call(
        text_grad_kernel, (block,), text_raw, home, forward, backward, *arrived, far=(1, 2, 3)
    )
    return (grad_weight, grad_features, grad_text)


def solution(mesh):
    fine = Mesh(mesh.devices.reshape(SPLIT), FINE)
    rows = P(FINE, None)
    return jax.shard_map(
        body,
        mesh=fine,
        in_specs=(rows, P(), rows, P(FINE)),
        out_specs=(P(), rows, rows),
        check_vma=False,
    )
```

```python
import functools

import jax
import jax.numpy as jnp
from jax import lax
from jax.experimental import pallas as pl
from jax.experimental.pallas import tpu as pltpu
from jax.sharding import Mesh, PartitionSpec as P

SCALE = 100.0
EPS = 1e-06
FINE = ("zh", "core", "zl", "x", "y")
SPLIT = (4, 2, 2, 4, 8)
PLANE = ("x", "y")
COLUMN = ("zh", "zl")
TAIL = 16
EARLY = 64
MIB = 1 << 20
HEAVY = 1 << 36


def shifted(block, axis, distance):
    count = lax.axis_size(axis)
    return lax.ppermute(block, axis, [(i, (i + distance) % count) for i in range(count)])


def exchanged(block, axes):
    return lax.all_to_all(block, axes, split_axis=0, concat_axis=0, tiled=True)


def dot(a, b, da, db):
    return lax.dot_general(a, b, (((da,), (db,)), ((), ())), preferred_element_type=jnp.float32)


def call(kernel, outs, *args, scratch=(), flops=0, limit=16, light=False, far=(), far_outs=False):
    whole = pl.BlockSpec(memory_space=pltpu.VMEM)
    scalars = pl.BlockSpec(memory_space=pltpu.SMEM)
    hbm = pl.BlockSpec(memory_space=pltpu.HBM)
    size = 0 if light else sum(a.size * a.dtype.itemsize for a in (*args, *outs))
    args = [
        pltpu.with_memory_space_constraint(a, pltpu.HBM) if n in far else a
        for n, a in enumerate(args)
    ]
    staged = [args[n] for n in far] + (list(outs) if far_outs else [])

    def staging(*refs):
        refs = list(refs)
        sems = refs.pop() if staged else None
        count = len(refs) - len(staged)
        refs, buffers = refs[:count], refs[count:]
        moves = []
        for n, at in enumerate(far):
            moves.append(pltpu.make_async_copy(refs[at], buffers[n], sems.at[n]))
            refs[at] = buffers[n]
        for move in moves:
            move.start()
        for move in moves:
            move.wait()
        moves = []
        if far_outs:
            for n in range(len(far), len(staged)):
                at = len(args) + n - len(far)
                moves.append(pltpu.make_async_copy(buffers[n], refs[at], sems.at[n]))
                refs[at] = buffers[n]
        kernel(*refs)
        for move in moves:
            move.start()
        for move in moves:
            move.wait()

    buffers = [pltpu.VMEM(a.shape, a.dtype) for a in staged]
    if staged:
        buffers.append(pltpu.SemaphoreType.DMA((len(staged),)))
    return pl.pallas_call(
        staging,
        out_shape=[pltpu.HBM(a.shape, a.dtype) for a in outs] if far_outs else outs,
        in_specs=[
            scalars if a.shape == (2,) else hbm if n in far else whole for n, a in enumerate(args)
        ],
        out_specs=[hbm if far_outs else whole] * len(outs),
        scratch_shapes=[*scratch, *buffers],
        compiler_params=pltpu.CompilerParams(vmem_limit_bytes=limit * MIB),
        cost_estimate=pl.CostEstimate(flops=flops, bytes_accessed=size, transcendentals=0),
    )(*args)


def shape(dims, dtype):
    return jax.ShapeDtypeStruct(dims, dtype)


def text_kernel(text_ref, sent_ref):
    rows = text_ref.shape[0]
    text = text_ref[...].astype(jnp.float32)
    scale = lax.rsqrt(jnp.sum(text * text, axis=1, keepdims=True) + EPS)
    text = (text * scale).astype(jnp.bfloat16).astype(jnp.float32)
    largest = jnp.max(jnp.max(jnp.abs(text), axis=1, keepdims=True), axis=0, keepdims=True)
    power = jnp.floor(jnp.log2(jnp.maximum(largest, 1e-30))) - 13.0
    sent_ref[:rows, :] = (text * jnp.exp2(-power)).astype(jnp.bfloat16)
    tail = (sent_ref.shape[0] - rows, sent_ref.shape[1])
    sent_ref[rows:, :] = jnp.broadcast_to(power, tail).astype(jnp.bfloat16)


def text_block(held_ref, n, rows):
    start = n * (rows + TAIL)
    power = held_ref[start + rows : start + rows + TAIL, :128].astype(jnp.float32)
    return held_ref[start : start + rows, :], SCALE * jnp.exp2(power[:1, :1])


def audio_kernel(
    features_ref, weight_ref, own_ref, audio_ref, audio_b_ref, scale_ref, scores_ref
):
    rows = audio_ref.shape[0]
    proj = dot(features_ref[...], weight_ref[...], 1, 0)
    scale = lax.rsqrt(jnp.sum(proj * proj, axis=1, keepdims=True) + EPS)
    audio = proj * scale
    audio_b = audio.astype(jnp.bfloat16)
    audio_ref[...] = audio
    audio_b_ref[...] = audio_b
    scale_ref[...] = scale
    for n in range(scores_ref.shape[1] // rows):
        block, factor = text_block(own_ref, n, rows)
        scores_ref[:, n * rows : (n + 1) * rows] = factor * dot(audio_b, block, 1, 1)


def score_kernel(
    place_ref, audio_ref, audio_b_ref, scale_ref, features_ref, positive_ref, own_ref, other_ref,
    own_scores_ref, grad_ref, tiles_ref, sent_ref, scores_ref,
):
    core = place_ref[1]
    blocks, rows, _ = tiles_ref.shape
    chips = blocks // 2
    audio_b = audio_b_ref[...]
    for n in range(chips):
        block, factor = text_block(other_ref, n, rows)
        scores_ref[:, n * rows : (n + 1) * rows] = factor * dot(audio_b, block, 1, 1)
    step = 16
    ids = lax.broadcasted_iota(jnp.int32, (step, rows), 1)
    for r in range(0, rows, step):
        both = [own_scores_ref[r : r + step, :], scores_ref[r : r + step, :]]
        peak = jnp.maximum(*(jnp.max(scores, axis=1, keepdims=True) for scores in both))
        both = [jnp.exp(scores - peak) for scores in both]
        share = 1.0 / sum(jnp.sum(weights, axis=1, keepdims=True) for weights in both)
        positive = positive_ref[r : r + step, :]
        for n in range(blocks):
            column = core if n < chips else 1 - core
            first = ((n % chips) * 2 + column) * rows
            match = jnp.where(positive - first == ids, 1.0, 0.0)
            lanes = slice(n % chips * rows, (n % chips + 1) * rows)
            part = both[n // chips][:, lanes] * share - match
            tiles_ref[n, r : r + step, :] = part.astype(jnp.bfloat16)
    total = jnp.zeros(audio_ref.shape, jnp.float32)
    for n in range(blocks):
        block, factor = text_block(own_ref if n < chips else other_ref, n % chips, rows)
        total = total + factor * dot(tiles_ref[n], block, 1, 0)
    audio = audio_ref[...]
    along = jnp.sum(audio * total, axis=1, keepdims=True)
    grad = ((total - audio * along) * scale_ref[...]).astype(jnp.bfloat16)
    grad_ref[...] = grad
    half = features_ref.shape[1] // 2
    features = features_ref[:, pl.ds(pl.multiple_of((1 - core) * half, half), half)]
    sent_ref[:half, :] = dot(features, grad, 0, 0).astype(jnp.bfloat16)
    for n in range(chips):
        part = SCALE * dot(tiles_ref[chips + n], audio_b, 0, 0)
        sent_ref[half + n * rows : half + (n + 1) * rows, :] = part.astype(jnp.bfloat16)


def own_kernel(place_ref, features_ref, grad_ref, weight_ref):
    half = features_ref.shape[1] // 2
    features = features_ref[:, pl.ds(pl.multiple_of(place_ref[1] * half, half), half)]
    weight_ref[...] = dot(features, grad_ref[...], 0, 0)


def half_kernel(weight_ref, got_ref, half_ref):
    parts, rows, width = half_ref.shape
    total = weight_ref[...] + got_ref[: parts * rows, :].astype(jnp.float32)
    half_ref[...] = total.astype(jnp.bfloat16).reshape(parts, rows, width)


def features_kernel(grad_ref, weight_ref, out_ref):
    out_ref[...] = dot(grad_ref[...], weight_ref[...], 1, 1).astype(jnp.bfloat16)


def summed(place_ref, tiles_ref, audio_b_ref, got_ref, distance):
    chips, rows = tiles_ref.shape[0] // 2, tiles_ref.shape[2]
    to = lax.rem(place_ref[0] + distance, chips)
    start = pl.multiple_of(got_ref.shape[0] - chips * rows + to * rows, rows)
    part = SCALE * dot(tiles_ref[to], audio_b_ref[...], 0, 0)
    return part + got_ref[pl.ds(start, rows), :].astype(jnp.float32)


def early_kernel(place_ref, tiles_ref, audio_b_ref, got_ref, forward_ref, backward_ref):
    refs = (place_ref, tiles_ref, audio_b_ref, got_ref)
    rows = tiles_ref.shape[2]
    cut = rows // 2
    across = summed(*refs, 2).astype(jnp.bfloat16)
    forward_ref[:cut, :] = across[:cut]
    backward_ref[:cut, :] = across[cut:]
    forward_ref[cut:, :] = summed(*refs, 1)[rows - EARLY :].astype(jnp.bfloat16)
    backward_ref[cut:, :] = summed(*refs, 3)[:EARLY].astype(jnp.bfloat16)


def late_kernel(place_ref, tiles_ref, audio_b_ref, got_ref, ahead_ref, behind_ref, home_ref):
    refs = (place_ref, tiles_ref, audio_b_ref, got_ref)
    rows = tiles_ref.shape[2]
    ahead_ref[...] = summed(*refs, 1)[: rows - EARLY]
    behind_ref[...] = summed(*refs, 3)[EARLY:]
    home_ref[...] = summed(*refs, 0)


def relay_kernel(ahead_ref, behind_ref, forward_ref, backward_ref, to_next_ref, to_last_ref):
    late = ahead_ref.shape[0]
    cut = (late + EARLY) // 2
    forward = forward_ref[:cut, :].astype(jnp.float32)
    backward = backward_ref[:cut, :].astype(jnp.float32)
    to_next_ref[:cut, :] = (ahead_ref[:cut, :] + forward).astype(jnp.bfloat16)
    to_next_ref[cut:, :] = ahead_ref[cut:, :].astype(jnp.bfloat16)
    to_last_ref[: late - cut, :] = behind_ref[: late - cut, :].astype(jnp.bfloat16)
    to_last_ref[late - cut :, :] = (behind_ref[late - cut :, :] + backward).astype(jnp.bfloat16)


def fold_kernel(parts_ref, copies_ref):
    total = jnp.sum(parts_ref[...].astype(jnp.float32), axis=0).astype(jnp.bfloat16)
    for n in range(copies_ref.shape[0]):
        copies_ref[n] = total


def place_kernel(side, place_ref, half_ref, *refs):
    whole_ref, buffer, sems = refs[-3:]
    pieces = sems.shape[0]
    rows = half_ref.shape[0]
    step = rows // pieces
    first = lax.rem(place_ref[1] + side, 2) * rows
    moves = []
    for n in range(pieces):
        part = pl.ds(n * step, step)
        buffer[part, :] = half_ref[part, :].astype(jnp.float32)
        to = pl.ds(pl.multiple_of(first + n * step, step), step)
        moves.append(pltpu.make_async_copy(buffer.at[part, :], whole_ref.at[to, :], sems.at[n]))
        moves[-1].start()
    for move in moves:
        move.wait()


def placed(place, half, side, whole):
    rows, width = half.shape
    given = [] if whole is None else [whole]
    return pl.pallas_call(
        functools.partial(place_kernel, side),
        out_shape=shape((2 * rows, width), jnp.float32),
        in_specs=[
            pl.BlockSpec(memory_space=pltpu.SMEM),
            pl.BlockSpec(memory_space=pltpu.VMEM),
            *[pl.BlockSpec(memory_space=pl.ANY)] * len(given),
        ],
        out_specs=pl.BlockSpec(memory_space=pl.ANY),
        scratch_shapes=[pltpu.VMEM((rows, width), jnp.float32), pltpu.SemaphoreType.DMA((4,))],
        input_output_aliases={2: 0} if given else {},
        compiler_params=pltpu.CompilerParams(vmem_limit_bytes=8 * MIB),
        cost_estimate=pl.CostEstimate(
            flops=0, bytes_accessed=6 * rows * width, transcendentals=0
        ),
    )(place, half, *given)


def text_grad_kernel(
    text_ref, home_ref, forward_ref, backward_ref, next_ref, last_ref, grad_ref
):
    rows, late = home_ref.shape[0], next_ref.shape[0]
    home = home_ref[...]
    forward = forward_ref[rows // 2 :, :].astype(jnp.float32)
    backward = backward_ref[rows // 2 :, :].astype(jnp.float32)
    ahead, behind = next_ref[...].astype(jnp.float32), last_ref[...].astype(jnp.float32)
    first = home[:EARLY] + ahead[:EARLY] + backward
    middle = home[EARLY:late] + ahead[EARLY:] + behind[: late - EARLY]
    final = home[late:] + forward + behind[late - EARLY :]
    grad = jnp.concatenate([first, middle, final])
    text = text_ref[...].astype(jnp.float32)
    scale = lax.rsqrt(jnp.sum(text * text, axis=1, keepdims=True) + EPS)
    text = text * scale
    along = jnp.sum(text * grad, axis=1, keepdims=True)
    grad_ref[...] = (grad - text * along) * scale


def body(audio_features, proj_weight, text_raw, positive):
    rows, channels = audio_features.shape
    width = text_raw.shape[1]
    chips = lax.axis_size("zh")
    blocks = chips * lax.axis_size("core")
    place = jnp.stack([lax.axis_index("zh"), lax.axis_index("core")]).astype(jnp.int32)
    bf16, f32 = jnp.bfloat16, jnp.float32
    pair_flops = 2 * rows * rows * blocks * width
    half = channels // 2
    block = shape((rows, width), f32)
    block_b = shape((rows, width), bf16)
    early_b = shape((rows // 2 + EARLY, width), bf16)
    late, late_b = (shape((rows - EARLY, width), dtype) for dtype in (f32, bf16))

    (sent,) = call(text_kernel, (shape((rows + TAIL, width), bf16),), text_raw)
    own = lax.all_gather(sent.astype(jnp.float16), "zh", axis=0, tiled=True).astype(bf16)
    own, audio_features = lax.optimization_barrier((own, audio_features))
    other = shifted(own, "core", 1)
    audio, audio_b, scale, own_scores = call(
        audio_kernel,
        (block, block_b, shape((rows, 1), f32), shape((rows, chips * rows), f32)),
        audio_features,
        proj_weight,
        own,
        flops=2 * rows * channels * width,
    )
    proj_grad, tiles, sent = call(
        score_kernel,
        (block_b, shape((blocks, rows, rows), bf16), shape((half + chips * rows, width), bf16)),
        place,
        audio,
        audio_b,
        scale,
        audio_features,
        positive.reshape(rows, 1),
        own,
        other,
        own_scores,
        scratch=[pltpu.VMEM((rows, chips * rows), f32)],
        flops=3 * pair_flops,
        limit=20,
    )
    got = shifted(sent, "core", 1)
    (weight,) = call(
        own_kernel, (shape((half, width), f32),), place, audio_features, proj_grad, light=True
    )
    (grad_features,) = call(
        features_kernel, (shape((rows, channels), bf16),), proj_grad, proj_weight, light=True
    )
    got, weight, grad_features = lax.optimization_barrier((got, weight, grad_features))
    plane = lax.axis_size(PLANE)
    column = lax.axis_size(COLUMN)
    part = half // plane
    (parts,) = call(half_kernel, (shape((plane, part, width), bf16),), weight, got, far_outs=True)
    parts, got = lax.optimization_barrier((parts, got))
    parts = exchanged(parts, PLANE)
    forward, backward = call(
        early_kernel, (early_b, early_b), place, tiles, audio_b, got, flops=pair_flops // 4
    )
    forward = shifted(forward, "zh", 1)
    backward = shifted(backward, "zh", -1)
    ahead, behind, home = call(
        late_kernel,
        (late, late, block),
        place,
        tiles,
        audio_b,
        got,
        flops=pair_flops,
        far_outs=True,
    )
    parts, ahead, behind, home = lax.optimization_barrier((parts, ahead, behind, home))
    (parts,) = call(fold_kernel, (shape((column, part, width), bf16),), parts, far_outs=True)
    parts = exchanged(parts, COLUMN)
    to_next, to_last = call(
        relay_kernel,
        (late_b, late_b),
        ahead,
        behind,
        forward,
        backward,
        light=True,
        far=(0, 1, 2, 3),
        far_outs=True,
    )
    (parts,) = call(fold_kernel, (shape((plane, part, width), bf16),), parts, far_outs=True)
    weight_half = exchanged(parts, PLANE).reshape(half, width)
    arrived = [shifted(to_next, "zh", 1), shifted(to_last, "zh", -1)]
    (grad_text,) = call(
        text_grad_kernel,
        (block,),
        text_raw,
        home,
        forward,
        backward,
        *arrived,
        flops=HEAVY,
        far=(1, 2, 3),
    )
    weight_half, grad_text = lax.optimization_barrier((weight_half, grad_text))
    there = shifted(weight_half, "core", 1)
    grad_weight = placed(place, weight_half, 0, None)
    grad_weight = placed(place, there, 1, grad_weight)
    return (grad_weight, grad_features, grad_text)


def solution(mesh):
    fine = Mesh(mesh.devices.reshape(SPLIT), FINE)
    rows = P(FINE, None)
    return jax.shard_map(
        body,
        mesh=fine,
        in_specs=(rows, P(), rows, P(FINE)),
        out_specs=(P(), rows, rows),
        check_vma=False,
    )
```

```python
import functools

import jax
import jax.numpy as jnp
from jax import lax
from jax.experimental import pallas as pl
from jax.experimental.pallas import tpu as pltpu
from jax.sharding import Mesh, PartitionSpec as P

SCALE = 100.0
EPS = 1e-06
FINE = ("zh", "core", "zl", "x", "y")
SPLIT = (4, 2, 2, 4, 8)
PLANE = ("x", "y")
COLUMN = ("zh", "zl")
TAIL = 16
MIB = 1 << 20
HEAVY = 1 << 36


def shifted(block, axis, distance):
    count = lax.axis_size(axis)
    return lax.ppermute(block, axis, [(i, (i + distance) % count) for i in range(count)])


def exchanged(block, axes):
    return lax.all_to_all(block, axes, split_axis=0, concat_axis=0, tiled=True)


def dot(a, b, da, db):
    return lax.dot_general(a, b, (((da,), (db,)), ((), ())), preferred_element_type=jnp.float32)


def call(kernel, outs, *args, scratch=(), flops=0, limit=16, light=False, far=(), far_outs=False):
    whole = pl.BlockSpec(memory_space=pltpu.VMEM)
    scalars = pl.BlockSpec(memory_space=pltpu.SMEM)
    hbm = pl.BlockSpec(memory_space=pltpu.HBM)
    size = 0 if light else sum(a.size * a.dtype.itemsize for a in (*args, *outs))
    args = [
        pltpu.with_memory_space_constraint(a, pltpu.HBM) if n in far else a
        for n, a in enumerate(args)
    ]
    staged = [args[n] for n in far] + (list(outs) if far_outs else [])

    def staging(*refs):
        refs = list(refs)
        sems = refs.pop() if staged else None
        count = len(refs) - len(staged)
        refs, buffers = refs[:count], refs[count:]
        moves = []
        for n, at in enumerate(far):
            moves.append(pltpu.make_async_copy(refs[at], buffers[n], sems.at[n]))
            refs[at] = buffers[n]
        for move in moves:
            move.start()
        for move in moves:
            move.wait()
        moves = []
        if far_outs:
            for n in range(len(far), len(staged)):
                at = len(args) + n - len(far)
                moves.append(pltpu.make_async_copy(buffers[n], refs[at], sems.at[n]))
                refs[at] = buffers[n]
        kernel(*refs)
        for move in moves:
            move.start()
        for move in moves:
            move.wait()

    buffers = [pltpu.VMEM(a.shape, a.dtype) for a in staged]
    if staged:
        buffers.append(pltpu.SemaphoreType.DMA((len(staged),)))
    return pl.pallas_call(
        staging,
        out_shape=[pltpu.HBM(a.shape, a.dtype) for a in outs] if far_outs else outs,
        in_specs=[
            scalars if a.shape == (2,) else hbm if n in far else whole for n, a in enumerate(args)
        ],
        out_specs=[hbm if far_outs else whole] * len(outs),
        scratch_shapes=[*scratch, *buffers],
        compiler_params=pltpu.CompilerParams(vmem_limit_bytes=limit * MIB),
        cost_estimate=pl.CostEstimate(flops=flops, bytes_accessed=size, transcendentals=0),
    )(*args)


def shape(dims, dtype):
    return jax.ShapeDtypeStruct(dims, dtype)


def text_kernel(text_ref, sent_ref):
    rows = text_ref.shape[0]
    text = text_ref[...].astype(jnp.float32)
    scale = lax.rsqrt(jnp.sum(text * text, axis=1, keepdims=True) + EPS)
    text = (text * scale).astype(jnp.bfloat16).astype(jnp.float32)
    largest = jnp.max(jnp.max(jnp.abs(text), axis=1, keepdims=True), axis=0, keepdims=True)
    power = jnp.floor(jnp.log2(jnp.maximum(largest, 1e-30))) - 13.0
    sent_ref[:rows, :] = (text * jnp.exp2(-power)).astype(jnp.bfloat16)
    tail = (sent_ref.shape[0] - rows, sent_ref.shape[1])
    sent_ref[rows:, :] = jnp.broadcast_to(power, tail).astype(jnp.bfloat16)


def text_block(held_ref, n, rows):
    start = n * (rows + TAIL)
    power = held_ref[start + rows : start + rows + TAIL, :128].astype(jnp.float32)
    return held_ref[start : start + rows, :], SCALE * jnp.exp2(power[:1, :1])


def audio_kernel(
    features_ref, weight_ref, own_ref, audio_ref, audio_b_ref, scale_ref, scores_ref
):
    rows = audio_ref.shape[0]
    proj = dot(features_ref[...], weight_ref[...], 1, 0)
    scale = lax.rsqrt(jnp.sum(proj * proj, axis=1, keepdims=True) + EPS)
    audio = proj * scale
    audio_b = audio.astype(jnp.bfloat16)
    audio_ref[...] = audio
    audio_b_ref[...] = audio_b
    scale_ref[...] = scale
    for n in range(scores_ref.shape[1] // rows):
        block, factor = text_block(own_ref, n, rows)
        scores_ref[:, n * rows : (n + 1) * rows] = factor * dot(audio_b, block, 1, 1)


def score_kernel(
    place_ref, audio_ref, audio_b_ref, scale_ref, features_ref, positive_ref, own_ref, other_ref,
    own_scores_ref, grad_ref, tiles_ref, sent_ref, scores_ref,
):
    core = place_ref[1]
    blocks, rows, _ = tiles_ref.shape
    chips = blocks // 2
    audio_b = audio_b_ref[...]
    for n in range(chips):
        block, factor = text_block(other_ref, n, rows)
        scores_ref[:, n * rows : (n + 1) * rows] = factor * dot(audio_b, block, 1, 1)
    step = 16
    ids = lax.broadcasted_iota(jnp.int32, (step, rows), 1)
    for r in range(0, rows, step):
        both = [own_scores_ref[r : r + step, :], scores_ref[r : r + step, :]]
        peak = jnp.maximum(*(jnp.max(scores, axis=1, keepdims=True) for scores in both))
        both = [jnp.exp(scores - peak) for scores in both]
        share = 1.0 / sum(jnp.sum(weights, axis=1, keepdims=True) for weights in both)
        positive = positive_ref[r : r + step, :]
        for n in range(blocks):
            column = core if n < chips else 1 - core
            first = ((n % chips) * 2 + column) * rows
            match = jnp.where(positive - first == ids, 1.0, 0.0)
            lanes = slice(n % chips * rows, (n % chips + 1) * rows)
            part = both[n // chips][:, lanes] * share - match
            tiles_ref[n, r : r + step, :] = part.astype(jnp.bfloat16)
    total = jnp.zeros(audio_ref.shape, jnp.float32)
    for n in range(blocks):
        block, factor = text_block(own_ref if n < chips else other_ref, n % chips, rows)
        total = total + factor * dot(tiles_ref[n], block, 1, 0)
    audio = audio_ref[...]
    along = jnp.sum(audio * total, axis=1, keepdims=True)
    grad = ((total - audio * along) * scale_ref[...]).astype(jnp.bfloat16)
    grad_ref[...] = grad
    half = features_ref.shape[1] // 2
    features = features_ref[:, pl.ds(pl.multiple_of((1 - core) * half, half), half)]
    sent_ref[:half, :] = dot(features, grad, 0, 0).astype(jnp.bfloat16)
    for n in range(chips):
        part = SCALE * dot(tiles_ref[chips + n], audio_b, 0, 0)
        sent_ref[half + n * rows : half + (n + 1) * rows, :] = part.astype(jnp.bfloat16)


def own_kernel(place_ref, features_ref, grad_ref, weight_ref):
    half = features_ref.shape[1] // 2
    features = features_ref[:, pl.ds(pl.multiple_of(place_ref[1] * half, half), half)]
    weight_ref[...] = dot(features, grad_ref[...], 0, 0)


def half_kernel(weight_ref, got_ref, half_ref):
    parts, rows, width = half_ref.shape
    total = weight_ref[...] + got_ref[: parts * rows, :].astype(jnp.float32)
    half_ref[...] = total.astype(jnp.bfloat16).reshape(parts, rows, width)


def features_kernel(grad_ref, weight_ref, out_ref):
    out_ref[...] = dot(grad_ref[...], weight_ref[...], 1, 1).astype(jnp.bfloat16)


def summed(place_ref, tiles_ref, audio_b_ref, got_ref, distance):
    chips, rows = tiles_ref.shape[0] // 2, tiles_ref.shape[2]
    to = lax.rem(place_ref[0] + distance, chips)
    start = pl.multiple_of(got_ref.shape[0] - chips * rows + to * rows, rows)
    part = SCALE * dot(tiles_ref[to], audio_b_ref[...], 0, 0)
    return part + got_ref[pl.ds(start, rows), :].astype(jnp.float32)


def early_kernel(place_ref, tiles_ref, audio_b_ref, got_ref, across_ref, last_ref):
    refs = (place_ref, tiles_ref, audio_b_ref, got_ref)
    across_ref[...] = summed(*refs, 2).astype(jnp.bfloat16)
    last_ref[...] = summed(*refs, 3).astype(jnp.bfloat16)


def late_kernel(place_ref, tiles_ref, audio_b_ref, got_ref, ahead_ref, home_ref):
    refs = (place_ref, tiles_ref, audio_b_ref, got_ref)
    ahead_ref[...] = summed(*refs, 1)
    home_ref[...] = summed(*refs, 0)


def relay_kernel(ahead_ref, across_ref, to_next_ref):
    to_next_ref[...] = (ahead_ref[...] + across_ref[...].astype(jnp.float32)).astype(jnp.bfloat16)


def fold_kernel(parts_ref, copies_ref):
    total = jnp.sum(parts_ref[...].astype(jnp.float32), axis=0).astype(jnp.bfloat16)
    for n in range(copies_ref.shape[0]):
        copies_ref[n] = total


def place_kernel(side, place_ref, half_ref, *refs):
    whole_ref, buffer, sems = refs[-3:]
    pieces = sems.shape[0]
    rows = half_ref.shape[0]
    step = rows // pieces
    first = lax.rem(place_ref[1] + side, 2) * rows
    moves = []
    for n in range(pieces):
        part = pl.ds(n * step, step)
        buffer[part, :] = half_ref[part, :].astype(jnp.float32)
        to = pl.ds(pl.multiple_of(first + n * step, step), step)
        moves.append(pltpu.make_async_copy(buffer.at[part, :], whole_ref.at[to, :], sems.at[n]))
        moves[-1].start()
    for move in moves:
        move.wait()


def placed(place, half, side, whole):
    rows, width = half.shape
    given = [] if whole is None else [whole]
    return pl.pallas_call(
        functools.partial(place_kernel, side),
        out_shape=shape((2 * rows, width), jnp.float32),
        in_specs=[
            pl.BlockSpec(memory_space=pltpu.SMEM),
            pl.BlockSpec(memory_space=pltpu.VMEM),
            *[pl.BlockSpec(memory_space=pl.ANY)] * len(given),
        ],
        out_specs=pl.BlockSpec(memory_space=pl.ANY),
        scratch_shapes=[pltpu.VMEM((rows, width), jnp.float32), pltpu.SemaphoreType.DMA((4,))],
        input_output_aliases={2: 0} if given else {},
        compiler_params=pltpu.CompilerParams(vmem_limit_bytes=8 * MIB),
        cost_estimate=pl.CostEstimate(
            flops=0, bytes_accessed=6 * rows * width, transcendentals=0
        ),
    )(place, half, *given)


def text_grad_kernel(text_ref, home_ref, last_ref, next_ref, grad_ref):
    grad = home_ref[...] + (last_ref[...].astype(jnp.float32) + next_ref[...].astype(jnp.float32))
    text = text_ref[...].astype(jnp.float32)
    scale = lax.rsqrt(jnp.sum(text * text, axis=1, keepdims=True) + EPS)
    text = text * scale
    along = jnp.sum(text * grad, axis=1, keepdims=True)
    grad_ref[...] = (grad - text * along) * scale


def body(audio_features, proj_weight, text_raw, positive):
    rows, channels = audio_features.shape
    width = text_raw.shape[1]
    chips = lax.axis_size("zh")
    blocks = chips * lax.axis_size("core")
    place = jnp.stack([lax.axis_index("zh"), lax.axis_index("core")]).astype(jnp.int32)
    bf16, f32 = jnp.bfloat16, jnp.float32
    pair_flops = 2 * rows * rows * blocks * width
    half = channels // 2
    block = shape((rows, width), f32)
    block_b = shape((rows, width), bf16)

    (sent,) = call(text_kernel, (shape((rows + TAIL, width), bf16),), text_raw)
    own = lax.all_gather(sent.astype(jnp.float16), "zh", axis=0, tiled=True).astype(bf16)
    own, audio_features = lax.optimization_barrier((own, audio_features))
    other = shifted(own, "core", 1)
    audio, audio_b, scale, own_scores = call(
        audio_kernel,
        (block, block_b, shape((rows, 1), f32), shape((rows, chips * rows), f32)),
        audio_features,
        proj_weight,
        own,
        flops=2 * rows * channels * width,
    )
    proj_grad, tiles, sent = call(
        score_kernel,
        (block_b, shape((blocks, rows, rows), bf16), shape((half + chips * rows, width), bf16)),
        place,
        audio,
        audio_b,
        scale,
        audio_features,
        positive.reshape(rows, 1),
        own,
        other,
        own_scores,
        scratch=[pltpu.VMEM((rows, chips * rows), f32)],
        flops=3 * pair_flops,
        limit=20,
    )
    got = shifted(sent, "core", 1)
    (weight,) = call(
        own_kernel, (shape((half, width), f32),), place, audio_features, proj_grad, light=True
    )
    (grad_features,) = call(
        features_kernel, (shape((rows, channels), bf16),), proj_grad, proj_weight, light=True
    )
    got, weight, grad_features = lax.optimization_barrier((got, weight, grad_features))
    plane = lax.axis_size(PLANE)
    column = lax.axis_size(COLUMN)
    part = half // plane
    (parts,) = call(half_kernel, (shape((plane, part, width), bf16),), weight, got, far_outs=True)
    parts, got = lax.optimization_barrier((parts, got))
    parts = exchanged(parts, PLANE)
    across, last = call(
        early_kernel, (block_b, block_b), place, tiles, audio_b, got, flops=pair_flops // 4
    )
    across = shifted(across, "zh", 1)
    last = shifted(last, "zh", -1)
    ahead, home = call(
        late_kernel, (block, block), place, tiles, audio_b, got, flops=pair_flops, far_outs=True
    )
    parts, ahead, home = lax.optimization_barrier((parts, ahead, home))
    (parts,) = call(fold_kernel, (shape((column, part, width), bf16),), parts, far_outs=True)
    parts, ahead = lax.optimization_barrier((parts, ahead))
    parts = exchanged(parts, COLUMN)
    (to_next,) = call(
        relay_kernel, (block_b,), ahead, across, flops=HEAVY, far=(0, 1), far_outs=True
    )
    (parts,) = call(
        fold_kernel, (shape((plane, part, width), bf16),), parts, flops=HEAVY, far_outs=True
    )
    weight_half = exchanged(parts, PLANE).reshape(half, width)
    arrived = shifted(to_next, "zh", 1)
    (grad_text,) = call(
        text_grad_kernel, (block,), text_raw, home, last, arrived, flops=HEAVY, far=(1, 2)
    )
    weight_half, grad_text = lax.optimization_barrier((weight_half, grad_text))
    there = shifted(weight_half, "core", 1)
    grad_weight = placed(place, weight_half, 0, None)
    grad_weight = placed(place, there, 1, grad_weight)
    return (grad_weight, grad_features, grad_text)


def solution(mesh):
    fine = Mesh(mesh.devices.reshape(SPLIT), FINE)
    rows = P(FINE, None)
    return jax.shard_map(
        body,
        mesh=fine,
        in_specs=(rows, P(), rows, P(FINE)),
        out_specs=(P(), rows, rows),
        check_vma=False,
    )
```

```python
import functools

import jax
import jax.numpy as jnp
from jax import lax
from jax.experimental import pallas as pl
from jax.experimental.pallas import tpu as pltpu
from jax.sharding import Mesh, PartitionSpec as P

SCALE = 100.0
EPS = 1e-06
FINE = ("zh", "core", "zl", "x", "y")
SPLIT = (4, 2, 2, 4, 8)
PLANE = ("x", "y")
COLUMN = ("zh", "zl")
TAIL = 16
MIB = 1 << 20
HEAVY = 1 << 36


def shifted(block, axis, distance):
    count = lax.axis_size(axis)
    return lax.ppermute(block, axis, [(i, (i + distance) % count) for i in range(count)])


def exchanged(block, axes):
    return lax.all_to_all(block, axes, split_axis=0, concat_axis=0, tiled=True)


def dot(a, b, da, db):
    return lax.dot_general(a, b, (((da,), (db,)), ((), ())), preferred_element_type=jnp.float32)


def call(kernel, outs, *args, scratch=(), flops=0, limit=16, light=False, far=(), far_outs=False):
    whole = pl.BlockSpec(memory_space=pltpu.VMEM)
    scalars = pl.BlockSpec(memory_space=pltpu.SMEM)
    hbm = pl.BlockSpec(memory_space=pltpu.HBM)
    size = 0 if light else sum(a.size * a.dtype.itemsize for a in (*args, *outs))
    args = [
        pltpu.with_memory_space_constraint(a, pltpu.HBM) if n in far else a
        for n, a in enumerate(args)
    ]
    staged = [args[n] for n in far] + (list(outs) if far_outs else [])

    def staging(*refs):
        refs = list(refs)
        sems = refs.pop() if staged else None
        count = len(refs) - len(staged)
        refs, buffers = refs[:count], refs[count:]
        moves = []
        for n, at in enumerate(far):
            moves.append(pltpu.make_async_copy(refs[at], buffers[n], sems.at[n]))
            refs[at] = buffers[n]
        for move in moves:
            move.start()
        for move in moves:
            move.wait()
        moves = []
        if far_outs:
            for n in range(len(far), len(staged)):
                at = len(args) + n - len(far)
                moves.append(pltpu.make_async_copy(buffers[n], refs[at], sems.at[n]))
                refs[at] = buffers[n]
        kernel(*refs)
        for move in moves:
            move.start()
        for move in moves:
            move.wait()

    buffers = [pltpu.VMEM(a.shape, a.dtype) for a in staged]
    if staged:
        buffers.append(pltpu.SemaphoreType.DMA((len(staged),)))
    return pl.pallas_call(
        staging,
        out_shape=[pltpu.HBM(a.shape, a.dtype) for a in outs] if far_outs else outs,
        in_specs=[
            scalars if a.shape == (2,) else hbm if n in far else whole for n, a in enumerate(args)
        ],
        out_specs=[hbm if far_outs else whole] * len(outs),
        scratch_shapes=[*scratch, *buffers],
        compiler_params=pltpu.CompilerParams(vmem_limit_bytes=limit * MIB),
        cost_estimate=pl.CostEstimate(flops=flops, bytes_accessed=size, transcendentals=0),
    )(*args)


def shape(dims, dtype):
    return jax.ShapeDtypeStruct(dims, dtype)


def text_kernel(text_ref, sent_ref):
    rows = text_ref.shape[0]
    text = text_ref[...].astype(jnp.float32)
    scale = lax.rsqrt(jnp.sum(text * text, axis=1, keepdims=True) + EPS)
    text = (text * scale).astype(jnp.bfloat16).astype(jnp.float32)
    largest = jnp.max(jnp.max(jnp.abs(text), axis=1, keepdims=True), axis=0, keepdims=True)
    power = jnp.floor(jnp.log2(jnp.maximum(largest, 1e-30))) - 13.0
    sent_ref[:rows, :] = (text * jnp.exp2(-power)).astype(jnp.bfloat16)
    tail = (sent_ref.shape[0] - rows, sent_ref.shape[1])
    sent_ref[rows:, :] = jnp.broadcast_to(power, tail).astype(jnp.bfloat16)


def text_block(held_ref, n, rows):
    start = n * (rows + TAIL)
    power = held_ref[start + rows : start + rows + TAIL, :128].astype(jnp.float32)
    return held_ref[start : start + rows, :], SCALE * jnp.exp2(power[:1, :1])


def audio_kernel(
    features_ref, weight_ref, own_ref,
    audio_ref, audio_b_ref, scale_ref, weights_ref, peak_ref, sum_ref, scores_ref,
):
    rows = audio_ref.shape[0]
    proj = dot(features_ref[...], weight_ref[...], 1, 0)
    scale = lax.rsqrt(jnp.sum(proj * proj, axis=1, keepdims=True) + EPS)
    audio = proj * scale
    audio_b = audio.astype(jnp.bfloat16)
    audio_ref[...] = audio
    audio_b_ref[...] = audio_b
    scale_ref[...] = scale
    for n in range(scores_ref.shape[1] // rows):
        block, factor = text_block(own_ref, n, rows)
        scores_ref[:, n * rows : (n + 1) * rows] = factor * dot(audio_b, block, 1, 1)
    step = 16
    for r in range(0, rows, step):
        scores = scores_ref[r : r + step, :]
        peak = jnp.max(scores, axis=1, keepdims=True)
        weights = jnp.exp(scores - peak)
        weights_ref[r : r + step, :] = weights
        peak_ref[r : r + step, :] = peak
        sum_ref[r : r + step, :] = jnp.sum(weights, axis=1, keepdims=True)


def score_kernel(
    place_ref, audio_ref, audio_b_ref, scale_ref, features_ref, positive_ref, own_ref, other_ref,
    own_weights_ref, own_peak_ref, own_sum_ref, grad_ref, tiles_ref, sent_ref, scores_ref,
):
    core = place_ref[1]
    blocks, rows, _ = tiles_ref.shape
    chips = blocks // 2
    audio_b = audio_b_ref[...]
    for n in range(chips):
        block, factor = text_block(other_ref, n, rows)
        scores_ref[:, n * rows : (n + 1) * rows] = factor * dot(audio_b, block, 1, 1)
    step = 16
    ids = lax.broadcasted_iota(jnp.int32, (step, rows), 1)
    for r in range(0, rows, step):
        scores = scores_ref[r : r + step, :]
        own_peak = own_peak_ref[r : r + step, :]
        peak = jnp.maximum(own_peak, jnp.max(scores, axis=1, keepdims=True))
        other_weights = jnp.exp(scores - peak)
        factor = jnp.exp(own_peak - peak)
        total = factor * own_sum_ref[r : r + step, :] + jnp.sum(other_weights, axis=1, keepdims=True)
        both = [own_weights_ref[r : r + step, :], other_weights]
        shares = [factor / total, 1.0 / total]
        positive = positive_ref[r : r + step, :]
        for n in range(blocks):
            column = core if n < chips else 1 - core
            first = ((n % chips) * 2 + column) * rows
            match = jnp.where(positive - first == ids, 1.0, 0.0)
            lanes = slice(n % chips * rows, (n % chips + 1) * rows)
            part = both[n // chips][:, lanes] * shares[n // chips] - match
            tiles_ref[n, r : r + step, :] = part.astype(jnp.bfloat16)
    total = jnp.zeros(audio_ref.shape, jnp.float32)
    for n in range(blocks):
        block, factor = text_block(own_ref if n < chips else other_ref, n % chips, rows)
        total = total + factor * dot(tiles_ref[n], block, 1, 0)
    audio = audio_ref[...]
    along = jnp.sum(audio * total, axis=1, keepdims=True)
    grad = ((total - audio * along) * scale_ref[...]).astype(jnp.bfloat16)
    grad_ref[...] = grad
    half = features_ref.shape[1] // 2
    features = features_ref[:, pl.ds(pl.multiple_of((1 - core) * half, half), half)]
    sent_ref[:half, :] = dot(features, grad, 0, 0).astype(jnp.bfloat16)
    for n in range(chips):
        part = SCALE * dot(tiles_ref[chips + n], audio_b, 0, 0)
        sent_ref[half + n * rows : half + (n + 1) * rows, :] = part.astype(jnp.bfloat16)


def own_kernel(place_ref, features_ref, grad_ref, weight_ref):
    half = features_ref.shape[1] // 2
    features = features_ref[:, pl.ds(pl.multiple_of(place_ref[1] * half, half), half)]
    weight_ref[...] = dot(features, grad_ref[...], 0, 0)


def half_kernel(weight_ref, got_ref, half_ref):
    parts, rows, width = half_ref.shape
    total = weight_ref[...] + got_ref[: parts * rows, :].astype(jnp.float32)
    half_ref[...] = total.astype(jnp.bfloat16).reshape(parts, rows, width)


def features_kernel(grad_ref, weight_ref, out_ref):
    out_ref[...] = dot(grad_ref[...], weight_ref[...], 1, 1).astype(jnp.bfloat16)


def summed(place_ref, tiles_ref, audio_b_ref, got_ref, distance):
    chips, rows = tiles_ref.shape[0] // 2, tiles_ref.shape[2]
    to = lax.rem(place_ref[0] + distance, chips)
    start = pl.multiple_of(got_ref.shape[0] - chips * rows + to * rows, rows)
    part = SCALE * dot(tiles_ref[to], audio_b_ref[...], 0, 0)
    return part + got_ref[pl.ds(start, rows), :].astype(jnp.float32)


def early_kernel(place_ref, tiles_ref, audio_b_ref, got_ref, across_ref, last_ref):
    refs = (place_ref, tiles_ref, audio_b_ref, got_ref)
    across_ref[...] = summed(*refs, 2).astype(jnp.bfloat16)
    last_ref[...] = summed(*refs, 3).astype(jnp.bfloat16)


def late_kernel(place_ref, tiles_ref, audio_b_ref, got_ref, ahead_ref, home_ref):
    refs = (place_ref, tiles_ref, audio_b_ref, got_ref)
    ahead_ref[...] = summed(*refs, 1)
    home_ref[...] = summed(*refs, 0)


def relay_kernel(ahead_ref, across_ref, to_next_ref):
    to_next_ref[...] = (ahead_ref[...] + across_ref[...].astype(jnp.float32)).astype(jnp.bfloat16)


def fold_kernel(parts_ref, copies_ref):
    total = jnp.sum(parts_ref[...].astype(jnp.float32), axis=0).astype(jnp.bfloat16)
    for n in range(copies_ref.shape[0]):
        copies_ref[n] = total


def place_kernel(side, place_ref, half_ref, *refs):
    whole_ref, buffer, sems = refs[-3:]
    pieces = sems.shape[0]
    rows = half_ref.shape[0]
    step = rows // pieces
    first = lax.rem(place_ref[1] + side, 2) * rows
    moves = []
    for n in range(pieces):
        part = pl.ds(n * step, step)
        buffer[part, :] = half_ref[part, :].astype(jnp.float32)
        to = pl.ds(pl.multiple_of(first + n * step, step), step)
        moves.append(pltpu.make_async_copy(buffer.at[part, :], whole_ref.at[to, :], sems.at[n]))
        moves[-1].start()
    for move in moves:
        move.wait()


def placed(place, half, side, whole):
    rows, width = half.shape
    given = [] if whole is None else [whole]
    return pl.pallas_call(
        functools.partial(place_kernel, side),
        out_shape=shape((2 * rows, width), jnp.float32),
        in_specs=[
            pl.BlockSpec(memory_space=pltpu.SMEM),
            pl.BlockSpec(memory_space=pltpu.VMEM),
            *[pl.BlockSpec(memory_space=pl.ANY)] * len(given),
        ],
        out_specs=pl.BlockSpec(memory_space=pl.ANY),
        scratch_shapes=[pltpu.VMEM((rows, width), jnp.float32), pltpu.SemaphoreType.DMA((4,))],
        input_output_aliases={2: 0} if given else {},
        compiler_params=pltpu.CompilerParams(vmem_limit_bytes=8 * MIB),
        cost_estimate=pl.CostEstimate(
            flops=0, bytes_accessed=6 * rows * width, transcendentals=0
        ),
    )(place, half, *given)


def text_grad_kernel(text_ref, home_ref, last_ref, next_ref, grad_ref):
    grad = home_ref[...] + (last_ref[...].astype(jnp.float32) + next_ref[...].astype(jnp.float32))
    text = text_ref[...].astype(jnp.float32)
    scale = lax.rsqrt(jnp.sum(text * text, axis=1, keepdims=True) + EPS)
    text = text * scale
    along = jnp.sum(text * grad, axis=1, keepdims=True)
    grad_ref[...] = (grad - text * along) * scale


def body(audio_features, proj_weight, text_raw, positive):
    rows, channels = audio_features.shape
    width = text_raw.shape[1]
    chips = lax.axis_size("zh")
    blocks = chips * lax.axis_size("core")
    place = jnp.stack([lax.axis_index("zh"), lax.axis_index("core")]).astype(jnp.int32)
    bf16, f32 = jnp.bfloat16, jnp.float32
    pair_flops = 2 * rows * rows * blocks * width
    half = channels // 2
    block = shape((rows, width), f32)
    block_b = shape((rows, width), bf16)

    (sent,) = call(text_kernel, (shape((rows + TAIL, width), bf16),), text_raw, far=(0,))
    own = lax.all_gather(sent.astype(jnp.float16), "zh", axis=0, tiled=True).astype(bf16)
    own, audio_features = lax.optimization_barrier((own, audio_features))
    other = shifted(own, "core", 1)
    row_f = shape((rows, 1), f32)
    audio, audio_b, scale, *own_terms = call(
        audio_kernel,
        (block, block_b, row_f, shape((rows, chips * rows), f32), row_f, row_f),
        audio_features,
        proj_weight,
        own,
        scratch=[pltpu.VMEM((rows, chips * rows), f32)],
        flops=2 * rows * channels * width,
    )
    proj_grad, tiles, sent = call(
        score_kernel,
        (block_b, shape((blocks, rows, rows), bf16), shape((half + chips * rows, width), bf16)),
        place,
        audio,
        audio_b,
        scale,
        audio_features,
        positive.reshape(rows, 1),
        own,
        other,
        *own_terms,
        scratch=[pltpu.VMEM((rows, chips * rows), f32)],
        flops=3 * pair_flops,
        limit=20,
    )
    got = shifted(sent, "core", 1)
    (weight,) = call(
        own_kernel, (shape((half, width), f32),), place, audio_features, proj_grad, light=True
    )
    (grad_features,) = call(
        features_kernel, (shape((rows, channels), bf16),), proj_grad, proj_weight, light=True
    )
    got, weight, grad_features = lax.optimization_barrier((got, weight, grad_features))
    plane = lax.axis_size(PLANE)
    column = lax.axis_size(COLUMN)
    part = half // plane
    (parts,) = call(half_kernel, (shape((plane, part, width), bf16),), weight, got, far_outs=True)
    parts, got = lax.optimization_barrier((parts, got))
    parts = exchanged(parts, PLANE)
    across, last = call(
        early_kernel, (block_b, block_b), place, tiles, audio_b, got, flops=pair_flops // 4
    )
    across = shifted(across, "zh", 1)
    last = shifted(last, "zh", -1)
    ahead, home = call(
        late_kernel, (block, block), place, tiles, audio_b, got, flops=pair_flops, far_outs=True
    )
    parts, ahead, home = lax.optimization_barrier((parts, ahead, home))
    (parts,) = call(fold_kernel, (shape((column, part, width), bf16),), parts, far_outs=True)
    parts, ahead = lax.optimization_barrier((parts, ahead))
    parts = exchanged(parts, COLUMN)
    (to_next,) = call(
        relay_kernel, (block_b,), ahead, across, flops=HEAVY, far=(0, 1), far_outs=True
    )
    (parts,) = call(
        fold_kernel, (shape((plane, part, width), bf16),), parts, flops=HEAVY, far_outs=True
    )
    weight_half = exchanged(parts, PLANE).reshape(half, width)
    arrived = shifted(to_next, "zh", 1)
    (grad_text,) = call(
        text_grad_kernel, (block,), text_raw, home, last, arrived, flops=HEAVY, far=(1, 2)
    )
    weight_half, grad_text = lax.optimization_barrier((weight_half, grad_text))
    there = shifted(weight_half, "core", 1)
    grad_weight = placed(place, weight_half, 0, None)
    grad_weight = placed(place, there, 1, grad_weight)
    return (grad_weight, grad_features, grad_text)


def solution(mesh):
    fine = Mesh(mesh.devices.reshape(SPLIT), FINE)
    rows = P(FINE, None)
    return jax.shard_map(
        body,
        mesh=fine,
        in_specs=(rows, P(), rows, P(FINE)),
        out_specs=(P(), rows, rows),
        check_vma=False,
    )
```

```python
import functools

import jax
import jax.numpy as jnp
from jax import lax
from jax.experimental import pallas as pl
from jax.experimental.pallas import tpu as pltpu
from jax.sharding import Mesh, PartitionSpec as P

SCALE = 100.0
EPS = 1e-06
FINE = ("zh", "core", "zl", "x", "y")
SPLIT = (4, 2, 2, 4, 8)
PLANE = ("x", "y")
COLUMN = ("zh", "zl")
TAIL = 16
MIB = 1 << 20
HEAVY = 1 << 36


def shifted(block, axis, distance):
    count = lax.axis_size(axis)
    return lax.ppermute(block, axis, [(i, (i + distance) % count) for i in range(count)])


def exchanged(block, axes):
    return lax.all_to_all(block, axes, split_axis=0, concat_axis=0, tiled=True)


def dot(a, b, da, db):
    return lax.dot_general(a, b, (((da,), (db,)), ((), ())), preferred_element_type=jnp.float32)


def call(kernel, outs, *args, scratch=(), flops=0, limit=16, light=False, far=(), far_outs=False, raw=()):
    whole = pl.BlockSpec(memory_space=pltpu.VMEM)
    scalars = pl.BlockSpec(memory_space=pltpu.SMEM)
    hbm = pl.BlockSpec(memory_space=pltpu.HBM)
    size = 0 if light else sum(a.size * a.dtype.itemsize for a in (*args, *outs))
    args = [
        pltpu.with_memory_space_constraint(a, pltpu.HBM) if n in (*far, *raw) else a
        for n, a in enumerate(args)
    ]
    staged = [args[n] for n in far] + (list(outs) if far_outs else [])

    def staging(*refs):
        refs = list(refs)
        sems = refs.pop() if staged else None
        count = len(refs) - len(staged)
        refs, buffers = refs[:count], refs[count:]
        moves = []
        for n, at in enumerate(far):
            moves.append(pltpu.make_async_copy(refs[at], buffers[n], sems.at[n]))
            refs[at] = buffers[n]
        for move in moves:
            move.start()
        for move in moves:
            move.wait()
        moves = []
        if far_outs:
            for n in range(len(far), len(staged)):
                at = len(args) + n - len(far)
                moves.append(pltpu.make_async_copy(buffers[n], refs[at], sems.at[n]))
                refs[at] = buffers[n]
        kernel(*refs)
        for move in moves:
            move.start()
        for move in moves:
            move.wait()

    buffers = [pltpu.VMEM(a.shape, a.dtype) for a in staged]
    if staged:
        buffers.append(pltpu.SemaphoreType.DMA((len(staged),)))
    return pl.pallas_call(
        staging,
        out_shape=[pltpu.HBM(a.shape, a.dtype) for a in outs] if far_outs else outs,
        in_specs=[
            scalars if a.shape == (2,) else hbm if n in (*far, *raw) else whole for n, a in enumerate(args)
        ],
        out_specs=[hbm if far_outs else whole] * len(outs),
        scratch_shapes=[*scratch, *buffers],
        compiler_params=pltpu.CompilerParams(vmem_limit_bytes=limit * MIB),
        cost_estimate=pl.CostEstimate(flops=flops, bytes_accessed=size, transcendentals=0),
    )(*args)


def shape(dims, dtype):
    return jax.ShapeDtypeStruct(dims, dtype)


def text_kernel(text_ref, sent_ref):
    rows = text_ref.shape[0]
    text = text_ref[...].astype(jnp.float32)
    scale = lax.rsqrt(jnp.sum(text * text, axis=1, keepdims=True) + EPS)
    text = (text * scale).astype(jnp.bfloat16).astype(jnp.float32)
    largest = jnp.max(jnp.max(jnp.abs(text), axis=1, keepdims=True), axis=0, keepdims=True)
    power = jnp.floor(jnp.log2(jnp.maximum(largest, 1e-30))) - 13.0
    sent_ref[:rows, :] = (text * jnp.exp2(-power)).astype(jnp.bfloat16)
    tail = (sent_ref.shape[0] - rows, sent_ref.shape[1])
    sent_ref[rows:, :] = jnp.broadcast_to(power, tail).astype(jnp.bfloat16)


def text_block(held_ref, n, rows):
    start = n * (rows + TAIL)
    power = held_ref[start + rows : start + rows + TAIL, :128].astype(jnp.float32)
    return held_ref[start : start + rows, :], SCALE * jnp.exp2(power[:1, :1])


def audio_kernel(
    features_ref, weight_ref, own_ref,
    audio_ref, audio_b_ref, scale_ref, weights_ref, peak_ref, sum_ref, scores_ref,
):
    rows = audio_ref.shape[0]
    proj = dot(features_ref[...], weight_ref[...], 1, 0)
    scale = lax.rsqrt(jnp.sum(proj * proj, axis=1, keepdims=True) + EPS)
    audio = proj * scale
    audio_b = audio.astype(jnp.bfloat16)
    audio_ref[...] = audio
    audio_b_ref[...] = audio_b
    scale_ref[...] = scale
    for n in range(scores_ref.shape[1] // rows):
        block, factor = text_block(own_ref, n, rows)
        scores_ref[:, n * rows : (n + 1) * rows] = factor * dot(audio_b, block, 1, 1)
    step = 16
    for r in range(0, rows, step):
        scores = scores_ref[r : r + step, :]
        peak = jnp.max(scores, axis=1, keepdims=True)
        weights = jnp.exp(scores - peak)
        weights_ref[r : r + step, :] = weights
        peak_ref[r : r + step, :] = peak
        sum_ref[r : r + step, :] = jnp.sum(weights, axis=1, keepdims=True)


def score_kernel(
    place_ref, audio_ref, audio_b_ref, scale_ref, features_ref, positive_ref, own_ref, far_ref,
    own_weights_ref, own_peak_ref, own_sum_ref, grad_ref, tiles_ref, sent_ref, scores_ref,
    other_ref, sems,
):
    core = place_ref[1]
    blocks, rows, _ = tiles_ref.shape
    chips = blocks // 2
    fetches = []
    for n in range(chips):
        part = pl.ds(n * (rows + TAIL), rows + TAIL)
        fetches.append(
            pltpu.make_async_copy(far_ref.at[part, :], other_ref.at[part, :], sems.at[n])
        )
        fetches[n].start()
    audio_b = audio_b_ref[...]
    for n in range(chips):
        fetches[n].wait()
        block, factor = text_block(other_ref, n, rows)
        scores_ref[:, n * rows : (n + 1) * rows] = factor * dot(audio_b, block, 1, 1)
    step = 16
    ids = lax.broadcasted_iota(jnp.int32, (step, rows), 1)
    for r in range(0, rows, step):
        scores = scores_ref[r : r + step, :]
        own_peak = own_peak_ref[r : r + step, :]
        peak = jnp.maximum(own_peak, jnp.max(scores, axis=1, keepdims=True))
        other_weights = jnp.exp(scores - peak)
        factor = jnp.exp(own_peak - peak)
        total = factor * own_sum_ref[r : r + step, :] + jnp.sum(other_weights, axis=1, keepdims=True)
        both = [own_weights_ref[r : r + step, :], other_weights]
        shares = [factor / total, 1.0 / total]
        positive = positive_ref[r : r + step, :]
        for n in range(blocks):
            column = core if n < chips else 1 - core
            first = ((n % chips) * 2 + column) * rows
            match = jnp.where(positive - first == ids, 1.0, 0.0)
            lanes = slice(n % chips * rows, (n % chips + 1) * rows)
            part = both[n // chips][:, lanes] * shares[n // chips] - match
            tiles_ref[n, r : r + step, :] = part.astype(jnp.bfloat16)
    total = jnp.zeros(audio_ref.shape, jnp.float32)
    for n in range(blocks):
        block, factor = text_block(own_ref if n < chips else other_ref, n % chips, rows)
        total = total + factor * dot(tiles_ref[n], block, 1, 0)
    audio = audio_ref[...]
    along = jnp.sum(audio * total, axis=1, keepdims=True)
    grad = ((total - audio * along) * scale_ref[...]).astype(jnp.bfloat16)
    grad_ref[...] = grad
    half = features_ref.shape[1] // 2
    features = features_ref[:, pl.ds(pl.multiple_of((1 - core) * half, half), half)]
    sent_ref[:half, :] = dot(features, grad, 0, 0).astype(jnp.bfloat16)
    for n in range(chips):
        part = SCALE * dot(tiles_ref[chips + n], audio_b, 0, 0)
        sent_ref[half + n * rows : half + (n + 1) * rows, :] = part.astype(jnp.bfloat16)


def own_kernel(place_ref, features_ref, grad_ref, weight_ref):
    half = features_ref.shape[1] // 2
    features = features_ref[:, pl.ds(pl.multiple_of(place_ref[1] * half, half), half)]
    weight_ref[...] = dot(features, grad_ref[...], 0, 0)


def half_kernel(weight_ref, got_ref, half_ref):
    parts, rows, width = half_ref.shape
    total = weight_ref[...] + got_ref[: parts * rows, :].astype(jnp.float32)
    half_ref[...] = total.astype(jnp.bfloat16).reshape(parts, rows, width)


def features_kernel(grad_ref, weight_ref, out_ref):
    out_ref[...] = dot(grad_ref[...], weight_ref[...], 1, 1).astype(jnp.bfloat16)


def summed(place_ref, tiles_ref, audio_b_ref, got_ref, distance):
    chips, rows = tiles_ref.shape[0] // 2, tiles_ref.shape[2]
    to = lax.rem(place_ref[0] + distance, chips)
    start = pl.multiple_of(got_ref.shape[0] - chips * rows + to * rows, rows)
    part = SCALE * dot(tiles_ref[to], audio_b_ref[...], 0, 0)
    return part + got_ref[pl.ds(start, rows), :].astype(jnp.float32)


def early_kernel(place_ref, tiles_ref, audio_b_ref, got_ref, across_ref, last_ref):
    refs = (place_ref, tiles_ref, audio_b_ref, got_ref)
    across_ref[...] = summed(*refs, 2).astype(jnp.bfloat16)
    last_ref[...] = summed(*refs, 3).astype(jnp.bfloat16)


def late_kernel(place_ref, tiles_ref, audio_b_ref, got_ref, ahead_ref, home_ref):
    refs = (place_ref, tiles_ref, audio_b_ref, got_ref)
    ahead_ref[...] = summed(*refs, 1)
    home_ref[...] = summed(*refs, 0)


def relay_kernel(ahead_ref, across_ref, to_next_ref):
    to_next_ref[...] = (ahead_ref[...] + across_ref[...].astype(jnp.float32)).astype(jnp.bfloat16)


def fold_kernel(parts_ref, copies_ref):
    total = jnp.sum(parts_ref[...].astype(jnp.float32), axis=0).astype(jnp.bfloat16)
    for n in range(copies_ref.shape[0]):
        copies_ref[n] = total


def place_kernel(side, place_ref, half_ref, *refs):
    whole_ref, buffer, sems = refs[-3:]
    pieces = sems.shape[0]
    rows = half_ref.shape[0]
    step = rows // pieces
    first = lax.rem(place_ref[1] + side, 2) * rows
    moves = []
    for n in range(pieces):
        part = pl.ds(n * step, step)
        buffer[part, :] = half_ref[part, :].astype(jnp.float32)
        to = pl.ds(pl.multiple_of(first + n * step, step), step)
        moves.append(pltpu.make_async_copy(buffer.at[part, :], whole_ref.at[to, :], sems.at[n]))
        moves[-1].start()
    for move in moves:
        move.wait()


def placed(place, half, side, whole):
    rows, width = half.shape
    given = [] if whole is None else [whole]
    return pl.pallas_call(
        functools.partial(place_kernel, side),
        out_shape=shape((2 * rows, width), jnp.float32),
        in_specs=[
            pl.BlockSpec(memory_space=pltpu.SMEM),
            pl.BlockSpec(memory_space=pltpu.VMEM),
            *[pl.BlockSpec(memory_space=pl.ANY)] * len(given),
        ],
        out_specs=pl.BlockSpec(memory_space=pl.ANY),
        scratch_shapes=[pltpu.VMEM((rows, width), jnp.float32), pltpu.SemaphoreType.DMA((4,))],
        input_output_aliases={2: 0} if given else {},
        compiler_params=pltpu.CompilerParams(vmem_limit_bytes=8 * MIB),
        cost_estimate=pl.CostEstimate(
            flops=0, bytes_accessed=6 * rows * width, transcendentals=0
        ),
    )(place, half, *given)


def text_grad_kernel(text_ref, home_ref, last_ref, next_ref, grad_ref):
    grad = home_ref[...] + (last_ref[...].astype(jnp.float32) + next_ref[...].astype(jnp.float32))
    text = text_ref[...].astype(jnp.float32)
    scale = lax.rsqrt(jnp.sum(text * text, axis=1, keepdims=True) + EPS)
    text = text * scale
    along = jnp.sum(text * grad, axis=1, keepdims=True)
    grad_ref[...] = (grad - text * along) * scale


def body(audio_features, proj_weight, text_raw, positive):
    rows, channels = audio_features.shape
    width = text_raw.shape[1]
    chips = lax.axis_size("zh")
    blocks = chips * lax.axis_size("core")
    place = jnp.stack([lax.axis_index("zh"), lax.axis_index("core")]).astype(jnp.int32)
    bf16, f32 = jnp.bfloat16, jnp.float32
    pair_flops = 2 * rows * rows * blocks * width
    half = channels // 2
    block = shape((rows, width), f32)
    block_b = shape((rows, width), bf16)

    (sent,) = call(text_kernel, (shape((rows + TAIL, width), bf16),), text_raw, far=(0,))
    own = lax.all_gather(sent.astype(jnp.float16), "zh", axis=0, tiled=True).astype(bf16)
    own, audio_features = lax.optimization_barrier((own, audio_features))
    other = shifted(own, "core", 1)
    row_f = shape((rows, 1), f32)
    audio, audio_b, scale, *own_terms = call(
        audio_kernel,
        (block, block_b, row_f, shape((rows, chips * rows), f32), row_f, row_f),
        audio_features,
        proj_weight,
        own,
        scratch=[pltpu.VMEM((rows, chips * rows), f32)],
        flops=2 * rows * channels * width,
    )
    proj_grad, tiles, sent = call(
        score_kernel,
        (block_b, shape((blocks, rows, rows), bf16), shape((half + chips * rows, width), bf16)),
        place,
        audio,
        audio_b,
        scale,
        audio_features,
        positive.reshape(rows, 1),
        own,
        other,
        *own_terms,
        scratch=[
            pltpu.VMEM((rows, chips * rows), f32),
            pltpu.VMEM(other.shape, bf16),
            pltpu.SemaphoreType.DMA((chips,)),
        ],
        flops=3 * pair_flops,
        limit=20,
        raw=(7,),
    )
    got = shifted(sent, "core", 1)
    (weight,) = call(
        own_kernel, (shape((half, width), f32),), place, audio_features, proj_grad, light=True
    )
    (grad_features,) = call(
        features_kernel, (shape((rows, channels), bf16),), proj_grad, proj_weight, light=True
    )
    got, weight, grad_features = lax.optimization_barrier((got, weight, grad_features))
    plane = lax.axis_size(PLANE)
    column = lax.axis_size(COLUMN)
    part = half // plane
    (parts,) = call(half_kernel, (shape((plane, part, width), bf16),), weight, got, far_outs=True)
    parts, got = lax.optimization_barrier((parts, got))
    parts = exchanged(parts, PLANE)
    across, last = call(
        early_kernel, (block_b, block_b), place, tiles, audio_b, got, flops=pair_flops // 4
    )
    across = shifted(across, "zh", 1)
    last = shifted(last, "zh", -1)
    ahead, home = call(
        late_kernel, (block, block), place, tiles, audio_b, got, flops=pair_flops, far_outs=True
    )
    parts, ahead, home = lax.optimization_barrier((parts, ahead, home))
    (parts,) = call(fold_kernel, (shape((column, part, width), bf16),), parts, far_outs=True)
    parts, ahead = lax.optimization_barrier((parts, ahead))
    parts = exchanged(parts, COLUMN)
    (to_next,) = call(
        relay_kernel, (block_b,), ahead, across, flops=HEAVY, far=(0, 1), far_outs=True
    )
    (parts,) = call(
        fold_kernel, (shape((plane, part, width), bf16),), parts, flops=HEAVY, far_outs=True
    )
    weight_half = exchanged(parts, PLANE).reshape(half, width)
    arrived = shifted(to_next, "zh", 1)
    (grad_text,) = call(
        text_grad_kernel, (block,), text_raw, home, last, arrived, flops=HEAVY, far=(1, 2)
    )
    weight_half, grad_text = lax.optimization_barrier((weight_half, grad_text))
    there = shifted(weight_half, "core", 1)
    grad_weight = placed(place, weight_half, 0, None)
    grad_weight = placed(place, there, 1, grad_weight)
    return (grad_weight, grad_features, grad_text)


def solution(mesh):
    fine = Mesh(mesh.devices.reshape(SPLIT), FINE)
    rows = P(FINE, None)
    return jax.shard_map(
        body,
        mesh=fine,
        in_specs=(rows, P(), rows, P(FINE)),
        out_specs=(P(), rows, rows),
        check_vma=False,
    )
```
